32 devices in a mesh: seq: 4 (over z), heads: 8 (over y, x, core).
Axes of the slice: x: 2, y: 2, z: 4, core: 2. Of those that a mesh axis runs over, the one named last changes fastest.
Arguments:
- hidden_in: bfloat16 [1024, 4, 2048], P(('seq', 'heads')), may hold values from -6 to 6
- grad_out: bfloat16 [1024, 4, 2048], P(('seq', 'heads')), may hold values from -6 to 6
- lengths: int32 [4], replicated, may hold values from 512 to 1024, as said below
- norm_gain: bfloat16 [3, 2048], P(None, 'seq'), may hold values from 0.5 to 1.5
- w_z: bfloat16 [3, 2048, 4096], P(None, 'seq', 'heads'), may hold values from -0.125 to 0.125
- w_x: bfloat16 [3, 2048, 4096], P(None, 'seq', 'heads'), may hold values from -0.125 to 0.125
- w_bc: bfloat16 [3, 2048, 256], P(None, 'seq'), may hold values from -0.125 to 0.125
- w_dt: bfloat16 [3, 2048, 64], P(None, 'seq', 'heads'), may hold values from -0.125 to 0.125
- conv_x: float32 [3, 4, 4096], P(None, None, 'heads'), may hold values from -3 to 3
- conv_x_bias: float32 [3, 4096], P(None, 'heads'), may hold values from -2 to 2
- conv_bc: float32 [3, 4, 256], replicated, may hold values from -3 to 3
- conv_bc_bias: float32 [3, 256], replicated, may hold values from -2 to 2
- dt_bias: float32 [3, 64], P(None, 'heads'), may hold values from -7 to -2
- a_log: float32 [3, 64], P(None, 'heads'), may hold values from -2 to 1
- d_skip: float32 [3, 64], P(None, 'heads'), may hold values from 0.5 to 1.5
- y_gain: float32 [3, 4096], P(None, 'heads'), may hold values from 0.5 to 1.5
- w_out: bfloat16 [3, 4096, 2048], P(None, 'heads', 'seq'), may hold values from -0.09375 to 0.09375
Outputs:
- hidden_out: float32 [1024, 4, 2048], P(('seq', 'heads'))
- grad_in: float32 [1024, 4, 2048], P(('seq', 'heads'))
- d_norm_gain: float32 [3, 2048], P(None, 'seq')
- d_w_z: float32 [3, 2048, 4096], P(None, 'seq', 'heads')
- d_w_x: float32 [3, 2048, 4096], P(None, 'seq', 'heads')
- d_w_bc: float32 [3, 2048, 256], P(None, 'seq')
- d_w_dt: float32 [3, 2048, 64], P(None, 'seq', 'heads')
- d_conv_x: float32 [3, 4, 4096], P(None, None, 'heads')
- d_conv_x_bias: float32 [3, 4096], P(None, 'heads')
- d_conv_bc: float32 [3, 4, 256], replicated
- d_conv_bc_bias: float32 [3, 256], replicated
- d_dt_bias: float32 [3, 64], P(None, 'heads')
- d_a_log: float32 [3, 64], P(None, 'heads')
- d_d_skip: float32 [3, 64], P(None, 'heads')
- d_y_gain: float32 [3, 4096], P(None, 'heads')
- d_w_out: float32 [3, 4096, 2048], P(None, 'heads', 'seq')
The draws below stay inside these ranges and needn't reach their ends.
Inputs may be any that keep to these rules, and one draw needn't show every extreme that they name: `lengths`: one of the 4 sequences fills all 1024 positions; positions at or past a sequence's length are padding.
All inputs are finite; a program needn't handle non-finite values.
Results may differ from the reference program's by a relative error of at most 0.035.
Values may be sent and summed in bfloat16 or wider, within the bound.
No kernel may reach another device: no remote copies, remote signals or barrier semaphores. Data moves between devices by JAX's collectives and lax.ppermute only.
A program may use at most 256 MiB of HBM per device.

```python
import jax
import jax.numpy as jnp
from jax import lax

D = 2048
HEADS = 64
HEADDIM = 64
STATE = 128
CONV = 4
SPAN = 256
LAYERS = 3
MB = 4
INNER = 4096
SEQLEN = 1024
N_SEQ = 4


def draw_lengths(key, part):
    first_key = jax.random.fold_in(key, 11)
    second_key = jax.random.fold_in(key, 12)
    others = jax.random.randint(first_key, (MB,), SEQLEN // 2, SEQLEN + 1)
    chosen = jax.random.randint(second_key, (), 0, MB)
    return jnp.where(jnp.arange(MB) == chosen, SEQLEN, others).astype(jnp.int32)


def level_of(key, shape, split, smallest, top_value):
    def one(axis_at, shards_of):
        draws = jax.random.uniform(jax.random.fold_in(jax.random.fold_in(key, 6), axis_at), (shards_of,), jnp.float32, smallest / len(split), top_value / len(split))
        return jnp.repeat(jnp.exp(draws), shape[axis_at] // shards_of).reshape((-1,) + (1,) * (len(shape) - axis_at - 1))

    loudness = one(*split[0])
    for cut in split[1:]:
        loudness = loudness * one(*cut)
    return loudness


def bell_draw(own_key, dims, width, bound, split=(), dtype=jnp.bfloat16):
    result = width * jax.random.normal(own_key, dims, jnp.float32)
    if split:
        result = result * level_of(own_key, dims, split, -0.22, 0.18)
    return jnp.clip(result, -bound, bound).astype(dtype)


def setup_inputs(seed: int = 0) -> dict:
    keys = jax.random.split(jax.random.key(seed), 18)
    hidden_in = bell_draw(keys[0], (SEQLEN, MB, D), 1.0, 6.0, ((0, 32),))
    grad_out = bell_draw(keys[1], (SEQLEN, MB, D), 1.0, 6.0, ((0, 32),))
    lengths = draw_lengths(jax.random.fold_in(keys[17], 71), 0)
    norm_gain = jnp.clip(1.0 + 0.1 * jax.random.normal(keys[3], (LAYERS, D), jnp.float32), 0.5, 1.5).astype(jnp.bfloat16)
    w_z = bell_draw(keys[4], (LAYERS, D, INNER), D ** -0.5, 0.125, ((1, 4), (2, 8)))
    w_x = bell_draw(keys[5], (LAYERS, D, INNER), D ** -0.5, 0.125, ((1, 4), (2, 8)))
    w_bc = bell_draw(keys[6], (LAYERS, D, 2 * STATE), D ** -0.5, 0.125, ((1, 4),))
    w_dt = bell_draw(keys[7], (LAYERS, D, HEADS), D ** -0.5, 0.125, ((1, 4), (2, 8)))
    conv_x = bell_draw(keys[8], (LAYERS, CONV, INNER), 0.5, 3.0, ((2, 8),), jnp.float32)
    conv_x_bias = bell_draw(keys[9], (LAYERS, INNER), 0.3, 2.0, ((1, 8),), jnp.float32)
    conv_bc = bell_draw(keys[10], (LAYERS, CONV, 2 * STATE), 0.5, 3.0, (), jnp.float32)
    conv_bc_bias = bell_draw(keys[11], (LAYERS, 2 * STATE), 0.3, 2.0, (), jnp.float32)
    dt_bias = jnp.clip(-7.0 + 5.0 * jax.random.uniform(keys[12], (LAYERS, HEADS), jnp.float32) ** level_of(keys[12], (LAYERS, HEADS), ((1, 8),), -0.2, 0.2), -7.0, -2.0)
    a_log = jnp.clip(-2.0 + 3.0 * jax.random.uniform(keys[13], (LAYERS, HEADS), jnp.float32) ** level_of(keys[13], (LAYERS, HEADS), ((1, 8),), -0.2, 0.2), -2.0, 1.0)
    d_skip = jnp.clip(0.5 + 1.0 * jax.random.uniform(keys[14], (LAYERS, HEADS), jnp.float32) ** level_of(keys[14], (LAYERS, HEADS), ((1, 8),), -0.2, 0.2), 0.5, 1.5)
    y_gain = jnp.clip(1.0 + 0.1 * jax.random.normal(keys[15], (LAYERS, INNER), jnp.float32), 0.5, 1.5)
    w_out = bell_draw(keys[16], (LAYERS, INNER, D), INNER ** -0.5, 0.09375, ((1, 8), (2, 4)))
    return dict(hidden_in=hidden_in, grad_out=grad_out, lengths=lengths, norm_gain=norm_gain, w_z=w_z, w_x=w_x, w_bc=w_bc, w_dt=w_dt, conv_x=conv_x, conv_x_bias=conv_x_bias, conv_bc=conv_bc, conv_bc_bias=conv_bc_bias, dt_bias=dt_bias, a_log=a_log, d_skip=d_skip, y_gain=y_gain, w_out=w_out)


EPSILON = 1e-05
PRECISE = lax.Precision.HIGHEST

@jax.custom_vjp
def low(v):
    return lax.optimization_barrier(v.astype(jnp.bfloat16)).astype(jnp.float32)

@jax.custom_vjp
def low_back(v):
    return v

def low_keep(v):
    return (low(v), None)

def low_pass(kept, grad):
    return (grad,)

def back_keep(v):
    return (v, None)

def back_low(kept, grad):
    return (low(grad),)
low.defvjp(low_keep, low_pass)
low_back.defvjp(back_keep, back_low)

def matmul(first_mat, second_mat):
    return jnp.dot(first_mat, second_mat, precision=PRECISE, preferred_element_type=jnp.float32)

def one_layer(x_seq, weights, valid_rows):
    gain_row, gate_w, mixed_w, shared_w, raw_w, conv_xw, conv_xb, conv_bw, conv_bb, bias_dt, log_rate, skip_gain, gain_out, out_w = weights
    factor = lax.rsqrt(lax.optimization_barrier(jnp.mean(x_seq * x_seq, axis=-1, keepdims=True)) + EPSILON)
    normed = low(x_seq * factor * gain_row)
    gate_rows = low_back(matmul(normed, gate_w))
    mixed = low_back(matmul(normed, mixed_w))
    shared = matmul(normed, shared_w)
    raw_dt = low_back(matmul(normed, raw_w))
    feed = jnp.concatenate([mixed, shared], axis=-1)
    feed_ext = jnp.pad(feed, ((CONV - 1, 0), (0, 0)))
    kernel_w = jnp.concatenate([conv_xw, conv_bw], axis=-1)
    running = jnp.concatenate([conv_xb, conv_bb], axis=-1)
    for offset in range(CONV):
        running = running + kernel_w[offset] * feed_ext[offset:offset + SEQLEN]
    active = jax.nn.silu(running) * valid_rows[:, None]
    values = low(active[:, :INNER])
    key_rows = low(active[:, INNER:INNER + STATE])
    query_rows = low(active[:, INNER + STATE:])
    stepped = jax.nn.softplus(raw_dt + bias_dt) * valid_rows[:, None]
    value_heads = values.reshape(N_SEQ, SPAN, HEADS, HEADDIM)
    key_blocks = key_rows.reshape(N_SEQ, SPAN, STATE)
    query_blocks = query_rows.reshape(N_SEQ, SPAN, STATE)
    step_blocks = stepped.reshape(N_SEQ, SPAN, HEADS)
    rising = jnp.cumsum(jnp.exp(log_rate) * step_blocks, axis=1)
    scores = jnp.einsum('ktn,ksn->kts', query_blocks, key_blocks, precision=PRECISE)
    causal = jnp.arange(SPAN)[:, None] >= jnp.arange(SPAN)[None, :]
    levels = jnp.transpose(rising, (0, 2, 1))
    spread_gap = jnp.where(causal, levels[:, :, None, :] - levels[:, :, :, None], 0.0)
    decays = jnp.where(causal, jnp.exp(spread_gap), 0.0)
    mix = low(scores[:, None] * decays * jnp.transpose(step_blocks, (0, 2, 1))[:, :, None, :])
    diagonal = low_back(jnp.einsum('khts,kshp->kthp', mix, value_heads, precision=PRECISE))
    closing = rising[:, -1]
    fading = jnp.exp(-closing)
    weighting = jnp.exp(rising - closing[:, None]) * step_blocks
    local_state = jnp.einsum('ksh,kshp,ksn->khpn', weighting, value_heads, key_blocks, precision=PRECISE)

    def advance(carry, item):
        return (item[0][:, None, None] * carry + item[1], carry)
    ignored, carried = lax.scan(advance, jnp.zeros((HEADS, HEADDIM, STATE), jnp.float32), (fading, local_state))
    offdiag = jnp.exp(-rising)[..., None] * jnp.einsum('ktn,khpn->kthp', query_blocks, carried, precision=PRECISE)
    joined = (diagonal + offdiag + skip_gain[:, None] * value_heads).reshape(SEQLEN, INNER)
    gated = joined * jax.nn.silu(gate_rows)
    second = lax.rsqrt(lax.optimization_barrier(jnp.mean(gated * gated, axis=-1, keepdims=True)) + EPSILON)
    normal_out = low(gated * second * gain_out)
    return x_seq + low_back(matmul(normal_out, out_w))

def reference(hidden_in, grad_out, lengths, norm_gain, w_z, w_x, w_bc, w_dt, conv_x, conv_x_bias, conv_bc, conv_bc_bias, dt_bias, a_log, d_skip, y_gain, w_out):
    params = tuple((item.astype(jnp.float32) for item in (norm_gain, w_z, w_x, w_bc, w_dt, conv_x, conv_x_bias, conv_bc, conv_bc_bias, dt_bias, a_log, d_skip, y_gain, w_out)))
    inputs = jnp.transpose(hidden_in.astype(jnp.float32), (1, 0, 2))
    masks = (jnp.arange(SEQLEN)[None, :] < lengths[:, None]).astype(jnp.float32)

    def whole(seq_inputs, weights):

        def one_sequence(item):
            x_seq, valid_rows = item
            for layer_index in range(LAYERS):
                x_seq = one_layer(x_seq, tuple((member[layer_index] for member in weights)), valid_rows)
            return x_seq
        return lax.map(jax.checkpoint(one_sequence), (seq_inputs, masks))
    outputs, backward = jax.vjp(whole, inputs, params)
    d_inputs, d_params = backward(jnp.transpose(grad_out.astype(jnp.float32), (1, 0, 2)))
    return (jnp.transpose(outputs, (1, 0, 2)), jnp.transpose(d_inputs, (1, 0, 2)), d_params[0], d_params[1], d_params[2], d_params[3], d_params[4], d_params[5], d_params[6], d_params[7], d_params[8], d_params[9], d_params[10], d_params[11], d_params[12], d_params[13])
```

```python
import functools

import jax
import jax.numpy as jnp
from jax import lax
from jax.experimental import pallas as pl
from jax.experimental.pallas import tpu as pltpu
from jax.sharding import PartitionSpec as P

F32 = jnp.float32
BF = jnp.bfloat16
EPSILON = 1e-05
LANES = 128
HALO = 16
NN = ((1,), (0,))
NT = ((1,), (1,))
TN = ((0,), (0,))
GROUPS = 2
VMEM_BYTES = 56 * 1024 * 1024


def mm(a, b, dims=NN):
    return lax.dot_general(a, b, (dims, ((), ())), preferred_element_type=F32)


def smem():
    return pl.BlockSpec(memory_space=pltpu.SMEM)


def anywhere():
    return pl.BlockSpec(memory_space=pl.ANY)


def whole(a):
    rank = len(a.shape)
    return pl.BlockSpec(tuple(a.shape), lambda i: (0,) * rank)


def per_seq(a):
    rank = len(a.shape)
    return pl.BlockSpec((1,) + tuple(a.shape[1:]), lambda i: (i,) + (0,) * (rank - 1))


def sds(shape, dtype):
    return jax.ShapeDtypeStruct(shape, dtype)


class Line:
    def __init__(self):
        self.last = ()

    def call(self, body, grid, ins, in_specs, outs, out_specs, scratch=(), name=None, after=()):
        waits = tuple(self.last) + tuple(after)
        count, extra = len(ins), len(waits)
        made = len(outs)

        def kernel(*refs):
            body(*refs[:count], *refs[count + extra : count + extra + made], *refs[count + extra + made + 1 :])
            refs[count + extra + made][...] = jnp.zeros((8, LANES), F32)

        mark = sds((8, LANES), F32)
        *results, token = pl.pallas_call(
            kernel,
            grid=(grid,),
            in_specs=list(in_specs) + [anywhere()] * extra,
            out_specs=list(out_specs) + [whole(mark)],
            out_shape=list(outs) + [mark],
            scratch_shapes=list(scratch),
            compiler_params=pltpu.CompilerParams(vmem_limit_bytes=VMEM_BYTES),
            cost_estimate=pl.CostEstimate(flops=1, bytes_accessed=1, transcendentals=0),
            name=name,
        )(*ins, *waits)
        self.last = (token,)
        return results


def head_lanes(heads, width, parts):
    shape = (LANES, width)
    lane = lax.broadcasted_iota(jnp.int32, shape, 0)
    head = lax.broadcasted_iota(jnp.int32, shape, 1) // (width // heads)
    hit = lane == head
    for part in range(1, parts):
        hit = hit | (lane == head + part * heads)
    return hit.astype(F32).astype(BF)


def three_parts(per_head, heads):
    lane = lax.broadcasted_iota(jnp.int32, per_head.shape, 1)
    x = jnp.where(lane < heads, per_head, 0.0)
    high = x.astype(BF).astype(F32)
    rest = x - high
    middle = rest.astype(BF).astype(F32)
    packed = high + pltpu.roll(middle, heads, 1) + pltpu.roll(rest - middle, 2 * heads, 1)
    return packed.astype(BF)


def expand(per_head, width, size):
    heads = width // size
    return mm(three_parts(per_head, heads), head_lanes(heads, width, 3))


def collapse(wide, size):
    width = wide.shape[1]
    heads = width // size
    high = wide.astype(BF)
    low = (wide - high.astype(F32)).astype(BF)
    shape = (width, LANES)
    table = lax.broadcasted_iota(jnp.int32, shape, 0) // size == lax.broadcasted_iota(jnp.int32, shape, 1)
    table = table.astype(F32).astype(BF)
    return mm(high, table) + mm(low, table)


def running_sum(per_head, heads, back=False):
    made = mm(triangle(per_head.shape[0], back).astype(BF), three_parts(per_head, heads))
    made = made + pltpu.roll(made, LANES - heads, 1) + pltpu.roll(made, LANES - 2 * heads, 1)
    lane = lax.broadcasted_iota(jnp.int32, made.shape, 1)
    return jnp.where(lane < heads, made, 0.0)


def sigmoid(x):
    return 0.5 * jnp.tanh(0.5 * x) + 0.5


def softplus(x):
    return jnp.maximum(x, 0.0) + jnp.log1p(jnp.exp(-jnp.abs(x)))


def valid_column(info, lengths, seq, length):
    rows = lax.broadcasted_iota(jnp.int32, (length, 1), 0) + info[2]
    return (rows < lengths[seq]).astype(F32)


def triangle(length, flipped=False):
    a = lax.broadcasted_iota(jnp.int32, (length, length), 0)
    b = lax.broadcasted_iota(jnp.int32, (length, length), 1)
    return ((a <= b) if flipped else (a >= b)).astype(F32)


def split_two(x):
    high = x.astype(BF)
    return high, (x - high.astype(F32)).astype(BF)


def lane_pack(columns, rows):
    lane = lax.broadcasted_iota(jnp.int32, (rows, LANES), 1)
    out = jnp.zeros((rows, LANES), F32)
    for place, column in enumerate(columns):
        out = jnp.where(lane == place, column.astype(F32), out)
    return out.astype(BF)


def decay_blocks(rise, rise_rows, head, length):
    half = length // 2
    column = rise[:, head : head + 1]
    row = rise_rows[head : head + 1, :]
    low = lax.broadcasted_iota(jnp.int32, (half, half), 0) >= lax.broadcasted_iota(
        jnp.int32, (half, half), 1
    )
    top = jnp.where(low, jnp.exp(row[:, :half] - column[:half]), 0.0)
    left = jnp.exp(row[:, :half] - column[half:])
    right = jnp.where(low, jnp.exp(row[:, half:] - column[half:]), 0.0)
    return top, left, right


def norm_body(last, width, total, info, x, gain, *refs):
    pieces, (x_out, branch_out, normed_out, payload_out) = refs[:-4], refs[-4:]
    summed = pieces[0][0].astype(F32)
    for piece in pieces[1:]:
        summed = summed + piece[0].astype(F32)
    squares = summed[:, width : width + 1] + summed[:, width + 1 : width + 2]
    factor = lax.rsqrt(squares / total + EPSILON)
    branch = summed[:, :width] * factor
    x_new = x[0] + branch
    x_out[0] = x_new
    branch_out[0] = branch.astype(BF)
    q = lax.rsqrt(jnp.mean(x_new * x_new, axis=-1, keepdims=True) + EPSILON)
    normed_out[0] = (x_new * q * gain[...]).astype(BF)
    high, low = split_two(factor)
    payload_out[0] = lane_pack((high, low), summed.shape[0])


def first_norm_body(x, gain, normed_out):
    x_new = x[0]
    q = lax.rsqrt(jnp.mean(x_new * x_new, axis=-1, keepdims=True) + EPSILON)
    normed_out[0] = (x_new * q * gain[...]).astype(BF)


def back_payload(grad_low, branch, factor_lanes, out):
    width = grad_low.shape[1]
    dotted = jnp.sum(grad_low.astype(F32) * branch.astype(F32), axis=-1, keepdims=True)
    high, low = split_two(dotted)
    lane = lax.broadcasted_iota(jnp.int32, (grad_low.shape[0], LANES), 1)
    lanes = factor_lanes.astype(F32)
    lanes = jnp.where(lane == 2, high.astype(F32), lanes)
    lanes = jnp.where(lane == 3, low.astype(F32), lanes)
    out[0, :, :width] = grad_low
    out[0, :, width:] = lanes.astype(BF)


def first_back_body(grad, branch, factor_lanes, out):
    back_payload(grad[0], branch[0], factor_lanes[0], out)


def back_norm_body(width, x, gain, grad, branch, factor_lanes, *refs):
    pieces, (grad_out, payload_out, gain_out) = refs[:-3], refs[-3:]
    d_normed = pieces[0][0].astype(F32)
    for piece in pieces[1:]:
        d_normed = d_normed + piece[0].astype(F32)
    rows = x[0]
    q = lax.rsqrt(jnp.mean(rows * rows, axis=-1, keepdims=True) + EPSILON)
    scaled = d_normed * gain[...]
    cross = jnp.sum(scaled * rows, axis=-1, keepdims=True)
    grad_new = grad[0] + q * scaled - rows * (q * q * q * cross / width)
    grad_out[0] = grad_new
    gain_out[0] = jnp.broadcast_to(
        jnp.sum(d_normed * rows * q, axis=0, keepdims=True), gain_out.shape[1:]
    )
    back_payload(grad_new.astype(BF), branch[0], factor_lanes[0], payload_out)


def collect_body(n, nh, info, *refs):
    pieces, steps = refs[:nh], refs[nh : nh + n]
    shared_out, step_out = refs[nh + n :]
    here, place = info[0], info[1]
    for k in range(nh):
        owner = here ^ k
        for s in range(n):
            source = lax.rem(place - s + n, n)
            for layer in range(shared_out.shape[0]):
                shared_out[layer, source, owner] = pieces[k][s, layer]
    step_out[...] = jnp.zeros_like(step_out)
    rows = steps[0].shape[1]
    for s in range(n):
        source = lax.rem(place - s + n, n)
        wide = steps[s].shape[2]
        for layer in range(step_out.shape[0]):
            step_out[layer, 0:rows, pl.ds(pl.multiple_of(source * wide, wide), wide)] = steps[s][layer]


def project_body(nh, channels, info, *refs):
    pieces = refs[:nh]
    w_x, w_bc, w_dt = refs[nh : nh + 3]
    x_out, feed_out, raw_out = refs[nh + 3 :]
    own = pieces[0].shape[1]
    for k in range(nh):
        start = pl.multiple_of((info[0] ^ k) * own, own)
        x_out[0, pl.ds(start, own), :] = pieces[k][0]
    rows = x_out[0]
    feed_out[0, :, :channels] = mm(rows, flat_rows(w_x))
    feed_out[0, :, channels:] = mm(rows, w_bc[...])
    raw_out[0] = mm(rows, w_dt[...], NT)


def flat_rows(w):
    table = w[...]
    return table.reshape(table.shape[0] * table.shape[2], table.shape[3])


def gate_body(x, w_z, gate_out):
    gate_out[0] = mm(x[0], flat_rows(w_z)).astype(BF)


def rates_of(raw, head_params):
    lanes = head_params[2:3]
    return softplus(raw + head_params[0:1]) * lanes


def local_body(
    channels, size, taps, info, lengths, feed, raw, x_halo, w_x, w_bc, conv_w, head_params,
    chan, values_out, shared_out, rise_out, step_out, local_out, state_out, fade_out, halo_out,
    ext, halo_all,
):
    seq = pl.program_id(0)
    length = feed.shape[1]
    state = (feed.shape[2] - channels) // 2

    @pl.when(seq == 0)
    def _():
        halo_all[:, :channels] = mm(x_halo[...], flat_rows(w_x))
        halo_all[:, channels:] = mm(x_halo[...], w_bc[...])

    rim = halo_all[pl.ds(pl.multiple_of(seq * HALO, HALO), HALO), :]
    halo_out[0] = rim
    ext[:HALO] = rim
    ext[HALO:] = feed[0]
    valid = valid_column(info, lengths, seq, length)
    pre = conv_w[taps : taps + 1]
    for k in range(taps):
        pre = pre + conv_w[k : k + 1] * ext[HALO - taps + 1 + k : HALO - taps + 1 + k + length]
    act = pre * sigmoid(pre) * valid
    low = act.astype(BF)
    values_out[0] = low[:, :channels]
    shared_out[0] = low[:, channels:]
    values = low[:, :channels].astype(F32)
    keys = low[:, channels : channels + state]
    queries = low[:, channels + state :]
    params = head_params[...]
    step = rates_of(raw[0], params) * valid
    rise = running_sum(jnp.exp(params[1:2]) * step, channels // size)
    rise_out[0] = rise
    step_out[0] = step
    closing = rise[length - 1 :, :]
    weight = jnp.exp(rise - closing) * step
    weighted = (expand(weight, channels, size) * values).astype(BF)
    state_out[0] = mm(keys, weighted, TN).astype(BF)
    fade_out[0] = expand(jnp.broadcast_to(jnp.exp(-closing), (8, LANES)), channels, size)
    scores = mm(queries, keys, NT)
    stepped = (values * expand(step, channels, size)).astype(BF)
    rise_rows = jnp.transpose(rise)
    half = length // 2
    group = LANES // size
    lane = lax.broadcasted_iota(jnp.int32, (length, LANES), 1) // size
    for pair in range(channels // LANES):
        block = stepped[:, pair * LANES : (pair + 1) * LANES]
        upper = jnp.zeros((half, LANES), F32)
        lower = jnp.zeros((half, LANES), F32)
        for inner in range(group):
            top, left, right = decay_blocks(rise, rise_rows, pair * group + inner, length)
            part = jnp.where(lane == inner, block, jnp.zeros_like(block))
            upper = upper + mm((scores[:half, :half] * top).astype(BF), part[:half])
            lower = lower + mm((scores[half:, :half] * left).astype(BF), part[:half])
            lower = lower + mm((scores[half:, half:] * right).astype(BF), part[half:])
        at = slice(pair * LANES, (pair + 1) * LANES)
        skipped = chan[1:2, at] * values[:, at]
        local_out[0, :half, at] = upper + skipped[:half]
        local_out[0, half:, at] = lower + skipped[half:]


def hop_body(arrived, own, fade, out):
    out[0] = (fade[0, 0:1] * arrived[0].astype(F32) + own[0].astype(F32)).astype(BF)


def received(parts):
    summed = parts[0][0]
    for part in parts[1:]:
        summed = summed + part[0]
    return summed


def scatter_rows(info, outs, table, own):
    for k, out in enumerate(outs):
        start = pl.multiple_of((info[0] ^ k) * own, own)
        out[0] = table[pl.ds(start, own), :].astype(BF)


def output_body(
    n, nh, size, info, local, gate, shared, rise, w_out, chan, *refs
):
    parts, rest = refs[: n - 1], refs[n - 1 :]
    full_out, carried_out = rest[:2]
    outs, table = rest[2 : 2 + nh], rest[2 + nh]
    carried = received(parts)
    carried_out[0] = carried
    length, channels = local.shape[1:]
    state = shared.shape[2] // 2
    queries = shared[0, :, state:]
    far = mm(queries, carried) * expand(jnp.exp(-rise[0]), channels, size)
    full = local[0] + far
    full_out[0] = full
    wide = gate[0].astype(F32)
    gated = full * wide * sigmoid(wide)
    squares = jnp.sum(gated * gated, axis=-1, keepdims=True)
    low = (gated * chan[0:1]).astype(BF)
    cols = w_out.shape[3]
    for s in range(n):
        table[:, s * cols : (s + 1) * cols] = mm(low, w_out[s, 0])
    high, rest_part = split_two(squares)
    table[:, n * cols :] = lane_pack((high, rest_part), length).astype(F32)
    scatter_rows(info, outs, table, length // nh)


def gate_back_body(
    n, nh, size, total, info, gate, full, values, shared, rise, w_out, chan, *refs
):
    pieces = refs[:nh]
    grad_out, d_gate_out, normal_out, d_full_out, state_out, sums_out, table = refs[nh:]
    seq = pl.program_id(0)
    own = pieces[0].shape[1]
    width = grad_out.shape[2]
    length, channels = gate.shape[1:]
    for k in range(nh):
        start = pl.multiple_of((info[0] ^ k) * own, own)
        grad_out[0, pl.ds(start, own), :] = pieces[k][0, :, :width]
        table[pl.ds(start, own), :] = pieces[k][0, :, width:].astype(F32)
    factor = table[:, 0:1] + table[:, 1:2]
    dotted = table[:, 2:3] + table[:, 3:4]
    cols = w_out.shape[3]
    d_normal = mm(grad_out[0, :, :cols], w_out[0, 0], NT)
    for s in range(1, n):
        d_normal = d_normal + mm(grad_out[0, :, s * cols : (s + 1) * cols], w_out[s, 0], NT)
    wide = gate[0].astype(F32)
    sig = sigmoid(wide)
    silu = wide * sig
    full_wide = full[0]
    gated = full_wide * silu
    gain = chan[0:1]
    normal = gated * factor
    normal_out[0] = (normal * gain).astype(BF)
    d_gated = factor * (d_normal * gain) - gated * (factor * factor * dotted / total)
    d_full = d_gated * silu
    d_gate_out[0] = (d_gated * full_wide * (sig * (1.0 + wide * (1.0 - sig)))).astype(BF)
    d_full_out[0] = d_full.astype(BF)
    state = shared.shape[2] // 2
    queries = shared[0, :, state:]
    spread = (d_full * expand(jnp.exp(-rise[0]), channels, size)).astype(BF)
    state_out[0] = mm(queries, spread, TN).astype(BF)

    @pl.when(seq == 0)
    def _():
        sums_out[...] = jnp.zeros_like(sums_out)

    sums_out[0:1] += jnp.sum(d_normal * normal, axis=0, keepdims=True)
    sums_out[1:2] += jnp.sum(d_full * values[0].astype(F32), axis=0, keepdims=True)


def mix_back_body(
    size, d_full, full, values, shared, rise, step, carried, chan, d_values_out, d_shared_out, rates_out
):
    length, channels = d_full.shape[1:]
    state = shared.shape[2] // 2
    keys, queries = shared[0, :, :state], shared[0, :, state:]
    d_low = d_full[0]
    d_wide = d_low.astype(F32)
    wide = values[0].astype(F32)
    rise_all, step_all = rise[0], step[0]
    spread = (d_wide * expand(jnp.exp(-rise_all), channels, size)).astype(BF)
    d_queries = mm(spread, carried[0], NT)
    step_wide = expand(step_all, channels, size)
    stepped = (wide * step_wide).astype(BF)
    scores = mm(queries, keys, NT)
    rise_rows = jnp.transpose(rise_all)
    half = length // 2
    group = LANES // size
    lane = lax.broadcasted_iota(jnp.int32, (length, LANES), 1) // size
    d_top = jnp.zeros((half, half), F32)
    d_left = jnp.zeros((half, half), F32)
    d_right = jnp.zeros((half, half), F32)
    blocks = []
    for pair in range(channels // LANES):
        at = slice(pair * LANES, (pair + 1) * LANES)
        block, d_block = stepped[:, at], d_low[:, at]
        first = jnp.zeros((half, LANES), F32)
        second = jnp.zeros((half, LANES), F32)
        for inner in range(group):
            top, left, right = decay_blocks(rise_all, rise_rows, pair * group + inner, length)
            part = jnp.where(lane == inner, d_block, jnp.zeros_like(d_block))
            d_top = d_top + mm(part[:half], block[:half], NT) * top
            d_left = d_left + mm(part[half:], block[:half], NT) * left
            d_right = d_right + mm(part[half:], block[half:], NT) * right
            first = first + mm((scores[:half, :half] * top).astype(BF), part[:half], TN)
            first = first + mm((scores[half:, :half] * left).astype(BF), part[half:], TN)
            second = second + mm((scores[half:, half:] * right).astype(BF), part[half:], TN)
        blocks.append(jnp.concatenate([first, second], axis=0))
    d_stepped = jnp.concatenate(blocks, axis=1)
    d_top, d_left, d_right = d_top.astype(BF), d_left.astype(BF), d_right.astype(BF)
    d_shared_out[0, :half, :state] = mm(d_top, queries[:half], TN) + mm(d_left, queries[half:], TN)
    d_shared_out[0, half:, :state] = mm(d_right, queries[half:], TN)
    d_shared_out[0, :half, state:] = d_queries[:half] + mm(d_top, keys[:half])
    d_shared_out[0, half:, state:] = d_queries[half:] + mm(d_left, keys[:half]) + mm(d_right, keys[half:])
    skip = chan[1:2]
    d_values_out[0] = (skip * d_wide + step_wide * d_stepped).astype(BF)
    d_step = collapse(wide * d_stepped, size)
    d_rise = collapse(stepped.astype(F32) * d_stepped - d_wide * (full[0] - skip * wide), size)
    rates_out[0, :, :LANES] = d_rise
    rates_out[0, :, LANES:] = d_step


def state_back_body(
    n, channels, size, taps, info, lengths, feed, raw, rim, values, shared, rise, step, carried,
    d_values_in, d_shared_in, rates, conv_w, head_params, *refs
):
    parts, rest = refs[: n - 1], refs[n - 1 :]
    d_pre_out, first_out, d_raw_out, conv_out, head_out, ext = rest
    seq = pl.program_id(0)
    after = received(parts)
    length = feed.shape[1]
    state = shared.shape[2] // 2
    keys = shared[0, :, :state]
    wide = values[0].astype(F32)
    rise_all, step_all = rise[0], step[0]
    closing = rise_all[length - 1 :, :]
    ratio = jnp.exp(rise_all - closing)
    weight_wide = expand(ratio * step_all, channels, size)
    reached = mm(keys, after)
    d_values = d_values_in[0].astype(F32) + weight_wide * reached
    d_keys = d_shared_in[0, :, :state] + mm((weight_wide * wide).astype(BF), after, NT)
    d_queries = d_shared_in[0, :, state:]
    d_ratio = collapse(wide * reached, size) * ratio
    d_step = rates[0, :, LANES:] + d_ratio
    moved = d_ratio * step_all
    fade_terms = jnp.sum(after.astype(F32) * carried[0].astype(F32), axis=0, keepdims=True)
    d_fade = collapse(jnp.broadcast_to(fade_terms, (8, channels)), size)[0:1]
    d_close = jnp.sum(moved, axis=0, keepdims=True) + d_fade * jnp.exp(-closing)
    last = lax.broadcasted_iota(jnp.int32, (length, LANES), 0) == length - 1
    d_rise = rates[0, :, :LANES] + moved - jnp.where(last, d_close, 0.0)
    gathered = running_sum(d_rise, channels // size, True)
    params = head_params[...]
    rate = jnp.exp(params[1:2])
    valid = valid_column(info, lengths, seq, length)
    d_raw = (d_step + rate * gathered) * sigmoid(raw[0] + params[0:1]) * valid * params[2:3]
    d_raw_out[0] = d_raw.astype(BF)
    ext[:HALO] = rim[0]
    ext[HALO:] = feed[0]

    @pl.when(seq == 0)
    def _():
        conv_out[...] = jnp.zeros_like(conv_out)
        head_out[...] = jnp.zeros_like(head_out)

    head_out[0:1] += jnp.sum(d_raw, axis=0, keepdims=True)
    head_out[1:2] += rate * jnp.sum(step_all * gathered, axis=0, keepdims=True)
    for start, stop, d_act in (
        (0, channels, d_values),
        (channels, channels + state, d_keys),
        (channels + state, channels + 2 * state, d_queries),
    ):
        at = slice(start, stop)
        pre = conv_w[taps : taps + 1, at]
        for k in range(taps):
            begin = HALO - taps + 1 + k
            pre = pre + conv_w[k : k + 1, at] * ext[begin : begin + length, at]
        sig = sigmoid(pre)
        d_pre = d_act * valid * (sig * (1.0 + pre * (1.0 - sig)))
        d_pre_out[0, :, at] = d_pre
        first_out[0, :, at] = d_pre[:8]
        for k in range(taps):
            begin = HALO - taps + 1 + k
            conv_out[k : k + 1, at] += jnp.sum(d_pre * ext[begin : begin + length, at], axis=0, keepdims=True)
        conv_out[taps : taps + 1, at] += jnp.sum(d_pre, axis=0, keepdims=True)


def spread_body(n, nh, channels, taps, info, d_pre, d_next, d_gate, d_raw, w_z, w_x, w_bc, w_dt, conv_w, *refs):
    d_feed_out, outs, ext, table = refs[0], refs[1 : 1 + nh], refs[1 + nh], refs[2 + nh]
    length = d_pre.shape[1]
    ext[:length] = d_pre[0]
    ext[length:] = d_next[0]
    d_feed = conv_w[taps - 1 : taps] * ext[:length]
    for k in range(taps - 1):
        d_feed = d_feed + conv_w[k : k + 1] * ext[taps - 1 - k : taps - 1 - k + length]
    low = d_feed.astype(BF)
    d_feed_out[0] = low
    cols = w_z.shape[2]
    for s in range(n):
        at = slice(s * cols, (s + 1) * cols)
        running = mm(d_gate[0], w_z[s, 0], NT)
        running = running + mm(low[:, :channels], w_x[s, 0], NT)
        running = running + mm(low[:, channels:], w_bc[at, :], NT)
        table[:, at] = running + mm(d_raw[0], w_dt[:, at])
    scatter_rows(info, outs, table, length // nh)


def weight_body(groups, *refs):
    normal, grad, x, d_gate = (refs[i * groups : (i + 1) * groups] for i in range(4))
    out = refs[4 * groups]
    for place, (lefts, rights) in enumerate(((normal, grad), (x, d_gate))):
        summed = mm(lefts[0][...], rights[0][...], TN)
        for left, right in zip(lefts[1:], rights[1:]):
            summed = summed + mm(left[...], right[...], TN)
        out[0, place] = summed.astype(BF)


def feed_weight_body(nh, groups, channels, info, *refs):
    x, d_feed, d_raw = (refs[i * groups : (i + 1) * groups] for i in range(3))
    x_out, dt_out, *outs = refs[3 * groups : 3 * groups + 2 + nh]
    table = refs[3 * groups + 2 + nh]
    for g in range(groups):
        left = x[g][...]
        made = mm(left, d_feed[g][...], TN)
        steps = mm(d_raw[g][...], left, TN)[: dt_out.shape[1]]
        if g == 0:
            table[...] = made
            dt_out[0] = steps
        else:
            table[...] += made
            dt_out[0] += steps
    x_out[0] = table[:, :channels].astype(BF)
    own = table.shape[0] // nh
    for k, out in enumerate(outs):
        start = pl.multiple_of((info[0] ^ k) * own, own)
        out[0] = table[pl.ds(start, own), channels:].astype(BF)


def place_body(nh, info, *refs):
    pieces, out = refs[:nh], refs[nh]
    for k in range(nh):
        for layer in range(out.shape[0]):
            out[layer, info[0] ^ k] = pieces[k][layer]


def gather_plan(layers):
    order = [(kind, layer) for layer in range(layers) for kind in ("x", "z", "o")]
    return [order[:1]] + [order[at : at + 2] for at in range(1, len(order), 2)]


def shards(
    hidden_in, grad_out, lengths, norm_gain, w_z, w_x, w_bc, w_dt, conv_x, conv_x_bias, conv_bc,
    conv_bc_bias, dt_bias, a_log, d_skip, y_gain, w_out,
):
    n, nh = lax.axis_size("seq"), lax.axis_size("heads")
    layers, depth, channels = w_z.shape
    width = depth * n
    heads_here = w_dt.shape[2]
    size = channels // heads_here
    both = w_bc.shape[2]
    state = both // 2
    taps = conv_x.shape[1]
    own, batches, _ = hidden_in.shape
    length = own * nh
    total = channels * nh
    feed_width = channels + both
    groups = GROUPS
    while batches % groups:
        groups //= 2
    part = batches // groups
    tokens = part * length
    here, place = lax.axis_index("heads"), lax.axis_index("seq")
    every = range(groups)
    infos = [jnp.stack([here, place, place * length, g * part]).astype(jnp.int32) for g in every]
    spans = [lengths[g * part : (g + 1) * part] for g in every]
    line = Line()
    call = line.call

    def flip(x, k):
        return lax.ppermute(x, "heads", [(i, i ^ k) for i in range(nh)])

    def along(x, s, keep=lambda i, j: True):
        pairs = [(i, (i + s) % n) for i in range(n) if keep(i, (i + s) % n)]
        return lax.ppermute(x, "seq", pairs)

    def gather_heads(x):
        evens = [x] + [flip(x, k) for k in range(2, nh, 2)]
        odds = [flip(piece, 1) for piece in evens]
        return [piece for pair in zip(evens, odds) for piece in pair]

    def scatter_heads(pieces):
        sums = [
            (pieces[k].astype(F32) + flip(pieces[k + 1], 1).astype(F32)).astype(BF)
            for k in range(0, nh, 2)
        ]
        return [sums[0]] + [flip(sums[k // 2], k) for k in range(2, nh, 2)]

    def gather_seq(x):
        return [x] + [along(x, s) for s in range(1, n)]

    def scatter_seq(a):
        own_part = lax.dynamic_index_in_dim(a, place, 0, False).astype(F32)
        for s in range(1, n):
            piece = lax.dynamic_index_in_dim(a, lax.rem(place + s, n), 0, False)
            own_part = own_part + along(piece, s).astype(F32)
        return own_part

    def in_order(parts):
        return jnp.roll(jnp.stack(parts[::-1]), place + 1, axis=0)

    weights = {}
    for batch in gather_plan(layers):
        sources = [{"x": w_x, "z": w_z, "o": w_out}[kind][layer] for kind, layer in batch]
        table = lax.all_gather(jnp.stack(sources), "seq", axis=0)
        for at, key in enumerate(batch):
            weights[key] = (table, at)

    def weight_spec(table, at):
        rank = len(table.shape)
        return pl.BlockSpec((table.shape[0], 1) + tuple(table.shape[2:]), lambda i: (0, at) + (0,) * (rank - 2))

    gains = in_order(gather_seq(norm_gain)).transpose(1, 0, 2).reshape(layers, 1, width).astype(F32)
    x_res = [hidden_in[:, g * part : (g + 1) * part].transpose(1, 0, 2).astype(F32) for g in every]
    normed = []
    for g in every:
        outs = [sds((part, own, width), BF)]
        normed += call(
            first_norm_body, part, [x_res[g], gains[0]], [per_seq(x_res[g]), whole(gains[0])], outs,
            [per_seq(outs[0])], name="first_norm",
        )
    rows_here = depth // nh
    share = lax.dynamic_slice_in_dim(w_bc, here * rows_here, rows_here, 1)
    share = jnp.stack(gather_seq(share))
    step_rows = jnp.pad(w_dt.transpose(0, 2, 1), ((0, 0), (0, -heads_here % 16), (0, 0)))
    shared_pieces = gather_heads(share)
    step_pieces = gather_seq(step_rows)
    collected = [sds((layers, n, nh, rows_here, both), BF), sds((layers, LANES, width), BF)]
    ins = [infos[0]] + shared_pieces + step_pieces
    shared_w, step_w = call(
        functools.partial(collect_body, n, nh), 1, ins, [smem()] + [whole(a) for a in ins[1:]],
        collected, [whole(a) for a in collected], name="collect",
    )
    shared_w = shared_w.reshape(layers, width, both)

    conv_all = jnp.concatenate([conv_x, conv_bc], axis=-1)
    bias_all = jnp.concatenate([conv_x_bias, conv_bc_bias], axis=-1)
    conv_all = jnp.concatenate(
        [conv_all, bias_all[:, None], jnp.zeros((layers, 7 - taps, feed_width), F32)], axis=1
    )
    lanes_used = (jnp.arange(LANES) < heads_here).astype(F32)
    pad_heads = lambda a: jnp.pad(a, ((0, 0), (0, LANES - heads_here)))
    head_all = jnp.stack(
        [pad_heads(dt_bias), pad_heads(a_log), jnp.broadcast_to(lanes_used, (layers, LANES))]
        + [jnp.zeros((layers, LANES), F32)] * 5,
        axis=1,
    )
    chan_all = jnp.stack(
        [y_gain, jnp.repeat(d_skip, size, axis=1)] + [jnp.zeros((layers, channels), F32)] * 6, axis=1
    )

    state_shape = sds((part, state, channels), BF)

    def first_hop(states, back):
        pair = (n - 1, n - 2) if back else (0, 1)
        return [lax.ppermute(states, "seq", [pair])]

    def next_hop(arrived, states, fade, back):
        at = len(arrived)
        ins = [arrived[-1], states, fade]
        (out,) = call(
            hop_body, part, ins, [per_seq(a) for a in ins], [state_shape], [per_seq(state_shape)], name="hop"
        )
        pair = (n - 1 - at, n - 2 - at) if back else (at, at + 1)
        arrived.append(lax.ppermute(out, "seq", [pair]))

    def rim_of(pieces):
        rows = sum(
            jnp.where((here ^ k) == nh - 1, pieces[k][:, own - HALO :].astype(F32), 0.0) for k in range(nh)
        ).astype(BF)
        return along(rows, 1, lambda i, j: j == i + 1).reshape(part * HALO, width)

    stored = []
    for layer in range(layers):
        conv_w, head_params, chan = conv_all[layer], head_all[layer], chan_all[layer]
        wbc_full, wdt_full = shared_w[layer], step_w[layer]
        w_x_full, w_z_full, w_o_full = weights["x", layer], weights["z", layer], weights["o", layer]
        saved = [dict(x_res=x_res[g]) for g in every]
        arrived, states, local = [None] * groups, [None] * groups, [None] * groups
        for g in every:
            it = saved[g]
            pieces = gather_heads(normed[g])
            x_halo = rim_of(pieces)
            ins = [infos[g]] + pieces + [w_x_full[0], wbc_full, wdt_full]
            outs = [
                sds((part, length, width), BF),
                sds((part, length, feed_width), F32),
                sds((part, length, LANES), F32),
            ]
            it["x_all"], it["feed"], it["raw"] = call(
                functools.partial(project_body, nh, channels), part, ins,
                [smem()] + [per_seq(a) for a in pieces] + [weight_spec(*w_x_full), whole(wbc_full), whole(wdt_full)],
                outs, [per_seq(a) for a in outs],
                name="project",
            )
            ins = [infos[g], spans[g], it["feed"], it["raw"], x_halo, w_x_full[0], wbc_full, conv_w, head_params, chan]
            outs = [
                sds((part, length, channels), BF),
                sds((part, length, both), BF),
                sds((part, length, LANES), F32),
                sds((part, length, LANES), F32),
                sds((part, length, channels), F32),
                state_shape,
                sds((part, 8, channels), F32),
                sds((part, HALO, feed_width), F32),
            ]
            specs = [per_seq(a) for a in outs]
            it["values"], it["shared"], it["rise"], it["step"], local[g], states[g], it["fade"], it["rim"] = call(
                functools.partial(local_body, channels, size, taps), part, ins,
                [smem(), smem(), per_seq(ins[2]), per_seq(ins[3]), whole(x_halo), weight_spec(*w_x_full)]
                + [whole(a) for a in ins[6:]],
                outs, specs,
                scratch=[
                    pltpu.VMEM((HALO + length, feed_width), F32),
                    pltpu.VMEM((part * HALO, feed_width), F32),
                ],
                name="local",
            )
            arrived[g] = first_hop(states[g], False)

        def gate(g):
            it = saved[g]
            outs = [sds((part, length, channels), BF)]
            (it["gate"],) = call(
                gate_body, part, [it["x_all"], w_z_full[0]], [per_seq(it["x_all"]), weight_spec(*w_z_full)],
                outs, [per_seq(outs[0])], name="gate",
            )

        def all_hops(fillers):
            for at in range(1, n - 1):
                for g in every:
                    next_hop(arrived[g], states[g], saved[g]["fade"], False)
                if fillers:
                    fillers.pop(0)()
            for filler in fillers:
                filler()

        all_hops([functools.partial(gate, g) for g in every])
        summed = [None] * groups
        for g in every:
            it = saved[g]
            ins = [infos[g], local[g], it["gate"], it["shared"], it["rise"], w_o_full[0], chan] + arrived[g]
            outs = [sds((part, length, channels), F32), sds((part, state, channels), BF)] + [
                sds((part, own, width + LANES), BF)
            ] * nh
            it["full"], it["carried"], *projected = call(
                functools.partial(output_body, n, nh, size), part, ins,
                [smem()] + [per_seq(a) for a in ins[1:5]] + [weight_spec(*w_o_full), whole(chan)]
                + [per_seq(a) for a in ins[7:]],
                outs, [per_seq(a) for a in outs],
                scratch=[pltpu.VMEM((length, width + LANES), F32)],
                name="output",
            )
            summed[g] = scatter_heads(projected)
        gain_next = gains[min(layer + 1, layers - 1)]
        for g in every:
            it = saved[g]
            ins = [infos[g], x_res[g], gain_next] + summed[g]
            outs = [
                sds((part, own, width), F32),
                sds((part, own, width), BF),
                sds((part, own, width), BF),
                sds((part, own, LANES), BF),
            ]
            x_res[g], it["branch"], normed[g], it["factor"] = call(
                functools.partial(norm_body, False, width, total), part, ins,
                [smem(), per_seq(ins[1]), whole(gain_next)] + [per_seq(a) for a in summed[g]],
                outs, [per_seq(a) for a in outs], name="norm",
            )
        stored.append(saved)

    grad_res, payload = [None] * groups, [None] * groups
    for g in every:
        top = stored[-1][g]
        grad_low = grad_out[:, g * part : (g + 1) * part].transpose(1, 0, 2)
        ins = [grad_low, top["branch"], top["factor"]]
        outs = [sds((part, own, width + LANES), BF)]
        (payload[g],) = call(
            first_back_body, part, ins, [per_seq(a) for a in ins], outs, [per_seq(a) for a in outs],
            name="first_back",
        )
        grad_res[g] = grad_low.astype(F32)
    flat = lambda a: a.reshape(tokens, a.shape[2])
    cut = pl.BlockSpec((tokens, depth), lambda i: (0, i))
    early_grads, late_grads = [None] * layers, [None] * layers
    shared_grads, small_grads = [None] * layers, [None] * layers
    for layer in reversed(range(layers)):
        conv_w, head_params, chan = conv_all[layer], head_all[layer], chan_all[layer]
        wbc_full, wdt_full = shared_w[layer], step_w[layer]
        w_x_full, w_z_full, w_o_full = weights["x", layer], weights["z", layer], weights["o", layer]
        saved = stored[layer]
        work = [dict() for g in every]
        for g in every:
            it, to = saved[g], work[g]
            pieces = gather_heads(payload[g])
            ins = [infos[g]] + [it[k] for k in ("gate", "full", "values", "shared", "rise")]
            ins += [w_o_full[0], chan] + pieces
            outs = [
                sds((part, length, width), BF),
                sds((part, length, channels), BF),
                sds((part, length, channels), BF),
                sds((part, length, channels), BF),
                state_shape,
                sds((8, channels), F32),
            ]
            specs = [per_seq(a) for a in outs[:5]] + [whole(outs[5])]
            to["grad"], to["d_gate"], to["normal"], to["d_full"], states[g], to["chan"] = call(
                functools.partial(gate_back_body, n, nh, size, total), part, ins,
                [smem()] + [per_seq(a) for a in ins[1:6]] + [weight_spec(*w_o_full), whole(chan)]
                + [per_seq(a) for a in pieces],
                outs, specs, scratch=[pltpu.VMEM((length, LANES), F32)],
                name="gate_back",
            )
            arrived[g] = first_hop(states[g], True)
        ins = [flat(to["normal"]) for to in work] + [flat(to["grad"]) for to in work]
        ins += [flat(it["x_all"]) for it in saved] + [flat(to["d_gate"]) for to in work]
        outs = [sds((n, 2, depth, channels), BF)]
        (early,) = call(
            functools.partial(weight_body, groups), n, ins,
            [whole(a) for a in ins[:groups]] + [cut] * (2 * groups) + [whole(a) for a in ins[3 * groups :]],
            outs, [per_seq(outs[0])], name="early_weights",
        )
        early_grads[layer] = lax.psum_scatter(early, "seq", scatter_dimension=0, tiled=False)

        def mix_back(g):
            it, to = saved[g], work[g]
            ins = [to["d_full"]] + [it[k] for k in ("full", "values", "shared", "rise", "step", "carried")] + [chan]
            outs = [
                sds((part, length, channels), BF),
                sds((part, length, both), F32),
                sds((part, length, 2 * LANES), F32),
            ]
            to["d_values"], to["d_shared"], to["d_rates"] = call(
                functools.partial(mix_back_body, size), part, ins,
                [per_seq(a) for a in ins[:-1]] + [whole(chan)], outs, [per_seq(a) for a in outs],
                name="mix_back",
                after=[late_grads[layer + 1]] if layer + 1 < layers and g == groups - 1 else [],
            )

        def state_back(g):
            it, to = saved[g], work[g]
            ins = [infos[g], spans[g]]
            ins += [it[k] for k in ("feed", "raw", "rim", "values", "shared", "rise", "step", "carried")]
            ins += [to["d_values"], to["d_shared"], to["d_rates"], conv_w, head_params] + arrived[g]
            outs = [
                sds((part, length, feed_width), F32),
                sds((part, 8, feed_width), F32),
                sds((part, length, LANES), BF),
                sds((8, feed_width), F32),
                sds((8, LANES), F32),
            ]
            to["d_pre"], first_rows, to["d_raw"], to["conv"], to["head"] = call(
                functools.partial(state_back_body, n, channels, size, taps), part, ins,
                [smem(), smem()] + [per_seq(a) for a in ins[2:13]] + [whole(conv_w), whole(head_params)]
                + [per_seq(a) for a in ins[15:]],
                outs, [per_seq(a) for a in outs[:3]] + [whole(a) for a in outs[3:]],
                scratch=[pltpu.VMEM((HALO + length, feed_width), F32)],
                name="state_back",
            )
            to["next"] = along(first_rows, -1, lambda i, j: j == i - 1)

        def spread(g):
            to = work[g]
            ins = [infos[g], to["d_pre"], to["next"], to["d_gate"], to["d_raw"]]
            ins += [w_z_full[0], w_x_full[0], wbc_full, wdt_full, conv_w]
            outs = [sds((part, length, feed_width), BF)] + [sds((part, own, width), BF)] * nh
            to["d_feed"], *pieces = call(
                functools.partial(spread_body, n, nh, channels, taps), part, ins,
                [smem()] + [per_seq(a) for a in ins[1:5]] + [weight_spec(*w_z_full), weight_spec(*w_x_full)]
                + [whole(a) for a in ins[7:]],
                outs, [per_seq(a) for a in outs],
                scratch=[pltpu.VMEM((length + 8, feed_width), F32), pltpu.VMEM((length, width), F32)],
                name="spread",
            )
            to["summed"] = scatter_heads(pieces)

        def all_hops_back(fillers):
            for at in range(1, n - 1):
                for g in every:
                    next_hop(arrived[g], states[g], saved[g]["fade"], True)
                if fillers:
                    fillers.pop(0)()
            for filler in fillers:
                filler()

        all_hops_back([functools.partial(mix_back, g) for g in every])
        for g in every:
            state_back(g)
        for g in every:
            spread(g)
        ins = [infos[0]] + [flat(it["x_all"]) for it in saved]
        ins += [flat(to["d_feed"]) for to in work] + [flat(to["d_raw"]) for to in work]
        outs = [sds((n, depth, channels), BF), sds((n, 16, depth), F32)] + [sds((n, rows_here, both), BF)] * nh
        d_wx, d_wdt, *shared_parts = call(
            functools.partial(feed_weight_body, nh, groups, channels), n, ins,
            [smem()] + [cut] * groups + [whole(a) for a in ins[1 + groups :]], outs, [per_seq(a) for a in outs],
            scratch=[pltpu.VMEM((depth, feed_width), F32)],
                name="late_weights",
        )
        late_grads[layer] = lax.psum_scatter(d_wx, "seq", scatter_dimension=0, tiled=False)
        below = stored[max(layer - 1, 0)]
        for g in every:
            it, to = saved[g], work[g]
            ins = [it["x_res"], gains[layer], grad_res[g], below[g]["branch"], below[g]["factor"]] + to["summed"]
            outs = [
                sds((part, own, width), F32),
                sds((part, own, width + LANES), BF),
                sds((part, 8, width), F32),
            ]
            grad_res[g], payload[g], to["gain"] = call(
                functools.partial(back_norm_body, width), part, ins,
                [per_seq(ins[0]), whole(ins[1])] + [per_seq(a) for a in ins[2:]],
                outs, [per_seq(a) for a in outs], name="back_norm",
                after=[early_grads[layer]] if g == groups - 1 and layer > 0 else [],
            )
        shared_grads[layer] = (shared_parts, d_wdt)
        small_grads[layer] = tuple(sum(to[k] for to in work) for k in ("chan", "conv", "head")) + (
            sum(jnp.sum(to["gain"][:, 0], axis=0) for to in work),
        )

    def sum_seq(a):
        return sum(gather_seq(a)[1:], a)

    def sum_heads(a):
        for bit in range(nh.bit_length() - 1):
            a = a + flip(a, 1 << bit)
        return a

    per_head = jnp.stack(
        [
            jnp.concatenate(
                [
                    s[0][:2].reshape(-1),
                    s[1][: taps + 1, :channels].reshape(-1),
                    s[2][:2].reshape(-1),
                    s[1][: taps + 1, channels:].reshape(-1),
                    s[3],
                ]
            )
            for s in small_grads
        ]
    )
    per_head = sum_seq(per_head)
    cut_at = 2 * channels + (taps + 1) * channels + 2 * LANES
    everywhere = sum_heads(per_head[:, cut_at:])
    chan_total = per_head[:, : 2 * channels].reshape(layers, 2, channels)
    conv_total = per_head[:, 2 * channels : (taps + 3) * channels].reshape(layers, taps + 1, channels)
    head_total = per_head[:, (taps + 3) * channels : cut_at].reshape(layers, 2, LANES)
    conv_shared = everywhere[:, : (taps + 1) * both].reshape(layers, taps + 1, both)
    gain_grad = lax.dynamic_slice_in_dim(everywhere[:, (taps + 1) * both :], place * depth, depth, 1)
    stacked = [jnp.stack([s[0][k] for s in shared_grads], axis=1) for k in range(nh)]
    in_plane = sum(a.astype(F32) for a in scatter_heads(stacked)).reshape(n, -1, both)
    steps = jnp.stack([s[1] for s in shared_grads], axis=1).reshape(n, -1, both)
    summed = scatter_seq(jnp.concatenate([in_plane, steps], axis=1))
    split_at = layers * rows_here
    pieces = gather_heads(summed[:split_at].reshape(layers, rows_here, both))
    step_sums = summed[split_at:].reshape(layers, 16, depth)
    ins = [infos[0]] + pieces
    outs = [sds((layers, nh, rows_here, both), F32)]
    (table,) = call(
        functools.partial(place_body, nh), 1, ins, [smem()] + [whole(a) for a in pieces],
        outs, [whole(outs[0])], name="place",
    )
    shared_grad = table.reshape(layers, depth, both)
    dt_grad = step_sums[:, :heads_here].transpose(0, 2, 1)
    back = lambda parts: jnp.concatenate(parts, axis=0).transpose(1, 0, 2)
    return (
        back(x_res),
        back(grad_res),
        gain_grad,
        jnp.stack([e[1] for e in early_grads]).astype(F32),
        jnp.stack(late_grads).astype(F32),
        shared_grad,
        dt_grad,
        conv_total[:, :taps],
        conv_total[:, taps],
        conv_shared[:, :taps],
        conv_shared[:, taps],
        head_total[:, 0, :heads_here],
        head_total[:, 1, :heads_here],
        jnp.sum(chan_total[:, 1].reshape(layers, heads_here, size), axis=-1),
        chan_total[:, 0],
        jnp.stack([e[0] for e in early_grads]).astype(F32),
    )


def solution(mesh):
    rows = P(("seq", "heads"), None, None)
    placed = (
        rows, rows, P(), P(None, "seq"), P(None, "seq", "heads"), P(None, "seq", "heads"),
        P(None, "seq", None), P(None, "seq", "heads"), P(None, None, "heads"), P(None, "heads"), P(), P(),
        P(None, "heads"), P(None, "heads"), P(None, "heads"), P(None, "heads"), P(None, "heads", "seq"),
    )
    made = (
        rows, rows, P(None, "seq"), P(None, "seq", "heads"), P(None, "seq", "heads"),
        P(None, "seq", None), P(None, "seq", "heads"), P(None, None, "heads"), P(None, "heads"), P(), P(),
        P(None, "heads"), P(None, "heads"), P(None, "heads"), P(None, "heads"), P(None, "heads", "seq"),
    )
    return jax.shard_map(shards, mesh=mesh, in_specs=placed, out_specs=made, check_vma=False)
```

```python
import functools

import jax
import jax.numpy as jnp
from jax import lax
from jax.experimental import pallas as pl
from jax.experimental.pallas import tpu as pltpu
from jax.sharding import PartitionSpec as P

F32 = jnp.float32
BF = jnp.bfloat16
EPSILON = 1e-05
LANES = 128
HALO = 8
RIM = 4
FADES = 16
NN = ((1,), (0,))
NT = ((1,), (1,))
TN = ((0,), (0,))
GROUPS = 1
EARLY_AT = ("state_back", 1)
LATE_AT = ("spread", 1)
VMEM_BYTES = 56 * 1024 * 1024


def mm(a, b, dims=NN):
    return lax.dot_general(a, b, (dims, ((), ())), preferred_element_type=F32)


def smem():
    return pl.BlockSpec(memory_space=pltpu.SMEM)


def anywhere():
    return pl.BlockSpec(memory_space=pl.ANY)


def whole(a):
    rank = len(a.shape)
    return pl.BlockSpec(tuple(a.shape), lambda i: (0,) * rank)


def per_seq(a):
    rank = len(a.shape)
    return pl.BlockSpec((1,) + tuple(a.shape[1:]), lambda i: (i,) + (0,) * (rank - 1))


def sds(shape, dtype):
    return jax.ShapeDtypeStruct(shape, dtype)


class Line:
    def __init__(self):
        self.last = ()

    def hand_on(self, arrays, after=()):
        shapes = [sds(a.shape, a.dtype) for a in arrays]
        return self.call(
            lambda *refs: None, 1, arrays, [anywhere()] * len(arrays), shapes, [anywhere()] * len(arrays),
            name="hand_on", after=after, aliases={i: i for i in range(len(arrays))},
        )

    def call(self, body, grid, ins, in_specs, outs, out_specs, scratch=(), name=None, after=(), aliases={}):
        waits = tuple(self.last) + tuple(after)
        count, extra = len(ins), len(waits)
        made = len(outs)

        def kernel(*refs):
            body(*refs[:count], *refs[count + extra : count + extra + made], *refs[count + extra + made + 1 :])
            refs[count + extra + made][...] = jnp.zeros((8, LANES), F32)

        mark = sds((8, LANES), F32)
        *results, token = pl.pallas_call(
            kernel,
            grid=(grid,),
            in_specs=list(in_specs) + [anywhere()] * extra,
            out_specs=list(out_specs) + [whole(mark)],
            out_shape=list(outs) + [mark],
            scratch_shapes=list(scratch),
            compiler_params=pltpu.CompilerParams(vmem_limit_bytes=VMEM_BYTES),
            cost_estimate=pl.CostEstimate(flops=1, bytes_accessed=1, transcendentals=0),
            input_output_aliases=aliases,
            name=name,
        )(*ins, *waits)
        self.last = (token,)
        return results


def head_lanes(heads, width, parts):
    shape = (LANES, width)
    lane = lax.broadcasted_iota(jnp.int32, shape, 0)
    head = lax.broadcasted_iota(jnp.int32, shape, 1) // (width // heads)
    hit = lane == head
    for part in range(1, parts):
        hit = hit | (lane == head + part * heads)
    return hit.astype(F32).astype(BF)


def three_parts(per_head, heads):
    lane = lax.broadcasted_iota(jnp.int32, per_head.shape, 1)
    x = jnp.where(lane < heads, per_head, 0.0)
    high = x.astype(BF).astype(F32)
    rest = x - high
    middle = rest.astype(BF).astype(F32)
    packed = high + pltpu.roll(middle, heads, 1) + pltpu.roll(rest - middle, 2 * heads, 1)
    return packed.astype(BF)


def expand(per_head, width, size):
    heads = width // size
    return mm(three_parts(per_head, heads), head_lanes(heads, width, 3))


def collapse(wide, size):
    width = wide.shape[1]
    heads = width // size
    high = wide.astype(BF)
    low = (wide - high.astype(F32)).astype(BF)
    shape = (width, LANES)
    table = lax.broadcasted_iota(jnp.int32, shape, 0) // size == lax.broadcasted_iota(jnp.int32, shape, 1)
    table = table.astype(F32).astype(BF)
    return mm(high, table) + mm(low, table)


def running_sum(per_head, heads, back=False):
    made = mm(triangle(per_head.shape[0], back).astype(BF), three_parts(per_head, heads))
    made = made + pltpu.roll(made, LANES - heads, 1) + pltpu.roll(made, LANES - 2 * heads, 1)
    lane = lax.broadcasted_iota(jnp.int32, made.shape, 1)
    return jnp.where(lane < heads, made, 0.0)


def sigmoid(x):
    return 0.5 * jnp.tanh(0.5 * x) + 0.5


def softplus(x):
    return jnp.maximum(x, 0.0) + jnp.log1p(jnp.exp(-jnp.abs(x)))


def valid_column(info, lengths, seq, length):
    rows = lax.broadcasted_iota(jnp.int32, (length, 1), 0) + info[2]
    return (rows < lengths[seq]).astype(F32)


def triangle(length, flipped=False):
    a = lax.broadcasted_iota(jnp.int32, (length, length), 0)
    b = lax.broadcasted_iota(jnp.int32, (length, length), 1)
    return ((a <= b) if flipped else (a >= b)).astype(F32)


def split_two(x):
    high = x.astype(BF)
    return high, (x - high.astype(F32)).astype(BF)


def lane_pack(columns, rows):
    lane = lax.broadcasted_iota(jnp.int32, (rows, LANES), 1)
    out = jnp.zeros((rows, LANES), F32)
    for place, column in enumerate(columns):
        out = jnp.where(lane == place, column.astype(F32), out)
    return out.astype(BF)


def decay_blocks(rise, rise_rows, head, length):
    half = length // 2
    column = rise[:, head : head + 1]
    row = rise_rows[head : head + 1, :]
    low = lax.broadcasted_iota(jnp.int32, (half, half), 0) >= lax.broadcasted_iota(
        jnp.int32, (half, half), 1
    )
    top = jnp.where(low, jnp.exp(row[:, :half] - column[:half]), 0.0)
    left = jnp.exp(row[:, :half] - column[half:])
    right = jnp.where(low, jnp.exp(row[:, half:] - column[half:]), 0.0)
    return top, left, right


def norm_body(last, width, total, info, x, gain, *refs):
    pieces, (x_out, branch_out, normed_out, payload_out) = refs[:-4], refs[-4:]
    summed = pieces[0][0].astype(F32)
    for piece in pieces[1:]:
        summed = summed + piece[0].astype(F32)
    squares = summed[:, width : width + 1] + summed[:, width + 1 : width + 2]
    factor = lax.rsqrt(squares / total + EPSILON)
    branch = summed[:, :width] * factor
    x_new = x[0] + branch
    x_out[0] = x_new
    branch_out[0] = branch.astype(BF)
    q = lax.rsqrt(jnp.mean(x_new * x_new, axis=-1, keepdims=True) + EPSILON)
    normed_out[0] = (x_new * q * gain[...]).astype(BF)
    high, low = split_two(factor)
    payload_out[0] = lane_pack((high, low), summed.shape[0])


def first_norm_body(x, gain, normed_out):
    x_new = x[0]
    q = lax.rsqrt(jnp.mean(x_new * x_new, axis=-1, keepdims=True) + EPSILON)
    normed_out[0] = (x_new * q * gain[...]).astype(BF)


def back_payload(grad_low, branch, factor_lanes, out):
    width = grad_low.shape[1]
    dotted = jnp.sum(grad_low.astype(F32) * branch.astype(F32), axis=-1, keepdims=True)
    high, low = split_two(dotted)
    lane = lax.broadcasted_iota(jnp.int32, (grad_low.shape[0], LANES), 1)
    lanes = factor_lanes.astype(F32)
    lanes = jnp.where(lane == 2, high.astype(F32), lanes)
    lanes = jnp.where(lane == 3, low.astype(F32), lanes)
    out[0, :, :width] = grad_low
    out[0, :, width:] = lanes.astype(BF)


def first_back_body(grad, branch, factor_lanes, out):
    back_payload(grad[0], branch[0], factor_lanes[0], out)


def back_norm_body(width, x, gain, grad, branch, factor_lanes, *refs):
    pieces, (grad_out, payload_out, gain_out) = refs[:-3], refs[-3:]
    d_normed = pieces[0][0].astype(F32)
    for piece in pieces[1:]:
        d_normed = d_normed + piece[0].astype(F32)
    rows = x[0]
    q = lax.rsqrt(jnp.mean(rows * rows, axis=-1, keepdims=True) + EPSILON)
    scaled = d_normed * gain[...]
    cross = jnp.sum(scaled * rows, axis=-1, keepdims=True)
    grad_new = grad[0] + q * scaled - rows * (q * q * q * cross / width)
    grad_out[0] = grad_new
    gain_out[0] = jnp.broadcast_to(
        jnp.sum(d_normed * rows * q, axis=0, keepdims=True), gain_out.shape[1:]
    )
    back_payload(grad_new.astype(BF), branch[0], factor_lanes[0], payload_out)


def collect_body(n, nh, info, *refs):
    pieces, steps = refs[:nh], refs[nh]
    shared_out, step_out = refs[nh + 1 :]
    step_out[...] = jnp.zeros_like(step_out)
    rows, wide = steps.shape[2:]
    for k in range(nh):
        for s in range(n):
            for layer in range(shared_out.shape[0]):
                shared_out[layer, s, info[0] ^ k] = pieces[k][s, layer]
    for s in range(n):
        for layer in range(step_out.shape[0]):
            step_out[layer, 0:rows, s * wide : (s + 1) * wide] = steps[s, layer]


def project_body(nh, channels, info, *refs):
    pieces = refs[:nh]
    w_x, w_bc, w_dt = refs[nh : nh + 3]
    x_out, feed_out, raw_out = refs[nh + 3 :]
    own = pieces[0].shape[1]
    for k in range(nh):
        start = pl.multiple_of((info[0] ^ k) * own, own)
        x_out[0, pl.ds(start, own), :] = pieces[k][0]
    rows = x_out[0]
    feed_out[0, :, :channels] = mm(rows, flat_rows(w_x))
    feed_out[0, :, channels:] = mm(rows, w_bc[...])
    raw_out[0] = mm(rows, w_dt[...], NT)


def flat_rows(w):
    table = w[...]
    return table.reshape(table.shape[0] * table.shape[2], table.shape[3])


def gate_body(x, w_z, gate_out):
    gate_out[0] = mm(x[0], flat_rows(w_z)).astype(BF)


def rates_of(raw, head_params):
    lanes = head_params[2:3]
    return softplus(raw + head_params[0:1]) * lanes


def local_body(
    channels, size, taps, info, lengths, feed, raw, x_halo, w_x, w_bc, conv_w, head_params,
    values_out, shared_out, rise_out, step_out, state_out, halo_out, ext, halo_all,
):
    seq = pl.program_id(0)
    length = feed.shape[1]
    state = (feed.shape[2] - channels) // 2

    @pl.when(seq == 0)
    def _():
        wide = mm(x_halo[...], flat_rows(w_x))
        narrow = mm(x_halo[...], w_bc[...])
        for m in range(halo_all.shape[0]):
            rows = slice(m * RIM, (m + 1) * RIM)
            halo_all[m, HALO - RIM :, :channels] = wide[rows]
            halo_all[m, HALO - RIM :, channels:] = narrow[rows]

    rim = halo_all[seq]
    halo_out[0] = rim
    ext[:HALO] = rim
    ext[HALO:] = feed[0]
    valid = valid_column(info, lengths, seq, length)
    pre = conv_w[taps : taps + 1]
    for k in range(taps):
        pre = pre + conv_w[k : k + 1] * ext[HALO - taps + 1 + k : HALO - taps + 1 + k + length]
    act = pre * sigmoid(pre) * valid
    low = act.astype(BF)
    values_out[0] = low[:, :channels]
    shared_out[0] = low[:, channels:]
    values = low[:, :channels].astype(F32)
    keys = low[:, channels : channels + state]
    params = head_params[...]
    step = rates_of(raw[0], params) * valid
    rise = running_sum(jnp.exp(params[1:2]) * step, channels // size)
    rise_out[0] = rise
    step_out[0] = step
    closing = rise[length - 1 :, :]
    weight = jnp.exp(rise - closing) * step
    weighted = (expand(weight, channels, size) * values).astype(BF)
    fade = expand(jnp.broadcast_to(jnp.exp(-closing), (FADES, LANES)), channels, size)
    put_state(state_out, mm(keys, weighted, TN), fade)


def mix_body(size, values, shared, rise_in, step, chan, local_out):
    length, channels = values.shape[1:]
    state = shared.shape[2] // 2
    keys, queries = shared[0, :, :state], shared[0, :, state:]
    wide = values[0].astype(F32)
    rise = rise_in[0]
    scores = mm(queries, keys, NT)
    stepped = (wide * expand(step[0], channels, size)).astype(BF)
    rise_rows = jnp.transpose(rise)
    half = length // 2
    group = LANES // size
    lane = lax.broadcasted_iota(jnp.int32, (length, LANES), 1) // size
    for pair in range(channels // LANES):
        block = stepped[:, pair * LANES : (pair + 1) * LANES]
        upper = jnp.zeros((half, LANES), F32)
        lower = jnp.zeros((half, LANES), F32)
        for inner in range(group):
            top, left, right = decay_blocks(rise, rise_rows, pair * group + inner, length)
            part = jnp.where(lane == inner, block, jnp.zeros_like(block))
            upper = upper + mm((scores[:half, :half] * top).astype(BF), part[:half])
            lower = lower + mm((scores[half:, :half] * left).astype(BF), part[:half])
            lower = lower + mm((scores[half:, half:] * right).astype(BF), part[half:])
        at = slice(pair * LANES, (pair + 1) * LANES)
        skipped = chan[1:2, at] * wide[:, at]
        local_out[0, :half, at] = upper + skipped[:half]
        local_out[0, half:, at] = lower + skipped[half:]


def put_state(out, made, fade=None):
    state, narrow = made.shape[0], out.shape[3]
    if fade is not None:
        high, low = split_two(fade)
        odd = lax.broadcasted_iota(jnp.int32, fade.shape, 0) % 2
        fade = jnp.where(odd == 0, high.astype(F32), low.astype(F32)).astype(BF)
    for j in range(out.shape[0]):
        at = slice(j * narrow, (j + 1) * narrow)
        out[j, 0, :state] = made[:, at].astype(BF)
        if fade is not None:
            out[j, 0, state:] = fade[:, at]


def get_state(part):
    pieces = [part[j, 0] for j in range(part.shape[0])]
    return pieces[0] if len(pieces) == 1 else jnp.concatenate(pieces, axis=1)


def chain_body(parts, carried, fades):
    state = carried.shape[2]
    for item in range(parts.shape[1]):
        running = jnp.zeros(carried.shape[2:], F32)
        for block in range(parts.shape[0]):
            carried[block, item] = running.astype(BF)
            rows = parts[block, item, state:].astype(F32)
            fade = rows[0:1] + rows[1:2]
            fades[block, item] = jnp.broadcast_to(fade, fades.shape[2:])
            running = fade * running + parts[block, item, :state].astype(F32)


def chain_back_body(parts, fades, carried):
    for item in range(parts.shape[1]):
        running = jnp.zeros(carried.shape[2:], F32)
        for block in range(parts.shape[0] - 1, -1, -1):
            carried[block, item] = running.astype(BF)
            running = fades[block, item, 0:1] * running + parts[block, item].astype(F32)


def scatter_rows(info, outs, table, own):
    for k, out in enumerate(outs):
        start = pl.multiple_of((info[0] ^ k) * own, own)
        out[0] = table[pl.ds(start, own), :].astype(BF)


def output_body(
    n, nh, size, info, local, gate, shared, rise, w_out, chan, arrived, *rest
):
    full_out, carried_out = rest[:2]
    outs, table = rest[2 : 2 + nh], rest[2 + nh]
    carried = get_state(arrived)
    carried_out[0] = carried
    length, channels = local.shape[1:]
    state = shared.shape[2] // 2
    queries = shared[0, :, state:]
    far = mm(queries, carried) * expand(jnp.exp(-rise[0]), channels, size)
    full = local[0] + far
    full_out[0] = full
    wide = gate[0].astype(F32)
    gated = full * wide * sigmoid(wide)
    squares = jnp.sum(gated * gated, axis=-1, keepdims=True)
    low = (gated * chan[0:1]).astype(BF)
    cols = w_out.shape[3]
    for s in range(n):
        table[:, s * cols : (s + 1) * cols] = mm(low, w_out[s, 0])
    high, rest_part = split_two(squares)
    table[:, n * cols :] = lane_pack((high, rest_part), length).astype(F32)
    scatter_rows(info, outs, table, length // nh)


def gate_back_body(
    n, nh, size, total, info, gate, full, values, shared, rise, w_out, chan, *refs
):
    pieces = refs[:nh]
    grad_out, d_gate_out, normal_out, d_full_out, state_out, sums_out, table = refs[nh:]
    seq = pl.program_id(0)
    own = pieces[0].shape[1]
    width = grad_out.shape[2]
    length, channels = gate.shape[1:]
    for k in range(nh):
        start = pl.multiple_of((info[0] ^ k) * own, own)
        grad_out[0, pl.ds(start, own), :] = pieces[k][0, :, :width]
        table[pl.ds(start, own), :] = pieces[k][0, :, width:].astype(F32)
    factor = table[:, 0:1] + table[:, 1:2]
    dotted = table[:, 2:3] + table[:, 3:4]
    cols = w_out.shape[3]
    d_normal = mm(grad_out[0, :, :cols], w_out[0, 0], NT)
    for s in range(1, n):
        d_normal = d_normal + mm(grad_out[0, :, s * cols : (s + 1) * cols], w_out[s, 0], NT)
    wide = gate[0].astype(F32)
    sig = sigmoid(wide)
    silu = wide * sig
    full_wide = full[0]
    gated = full_wide * silu
    gain = chan[0:1]
    normal = gated * factor
    normal_out[0] = (normal * gain).astype(BF)
    d_gated = factor * (d_normal * gain) - gated * (factor * factor * dotted / total)
    d_full = d_gated * silu
    d_gate_out[0] = (d_gated * full_wide * (sig * (1.0 + wide * (1.0 - sig)))).astype(BF)
    d_full_out[0] = d_full.astype(BF)
    state = shared.shape[2] // 2
    queries = shared[0, :, state:]
    spread = (d_full * expand(jnp.exp(-rise[0]), channels, size)).astype(BF)
    put_state(state_out, mm(queries, spread, TN))

    @pl.when(seq == 0)
    def _():
        sums_out[...] = jnp.zeros_like(sums_out)

    sums_out[0:1] += jnp.sum(d_normal * normal, axis=0, keepdims=True)
    sums_out[1:2] += jnp.sum(d_full * values[0].astype(F32), axis=0, keepdims=True)


def mix_back_body(
    size, d_full, full, values, shared, rise, step, carried, chan, d_values_out, d_shared_out, rates_out
):
    length, channels = d_full.shape[1:]
    state = shared.shape[2] // 2
    keys, queries = shared[0, :, :state], shared[0, :, state:]
    d_low = d_full[0]
    d_wide = d_low.astype(F32)
    wide = values[0].astype(F32)
    rise_all, step_all = rise[0], step[0]
    spread = (d_wide * expand(jnp.exp(-rise_all), channels, size)).astype(BF)
    d_queries = mm(spread, carried[0], NT)
    step_wide = expand(step_all, channels, size)
    stepped = (wide * step_wide).astype(BF)
    scores = mm(queries, keys, NT)
    rise_rows = jnp.transpose(rise_all)
    half = length // 2
    group = LANES // size
    lane = lax.broadcasted_iota(jnp.int32, (length, LANES), 1) // size
    d_top = jnp.zeros((half, half), F32)
    d_left = jnp.zeros((half, half), F32)
    d_right = jnp.zeros((half, half), F32)
    blocks = []
    for pair in range(channels // LANES):
        at = slice(pair * LANES, (pair + 1) * LANES)
        block, d_block = stepped[:, at], d_low[:, at]
        first = jnp.zeros((half, LANES), F32)
        second = jnp.zeros((half, LANES), F32)
        for inner in range(group):
            top, left, right = decay_blocks(rise_all, rise_rows, pair * group + inner, length)
            part = jnp.where(lane == inner, d_block, jnp.zeros_like(d_block))
            d_top = d_top + mm(part[:half], block[:half], NT) * top
            d_left = d_left + mm(part[half:], block[:half], NT) * left
            d_right = d_right + mm(part[half:], block[half:], NT) * right
            first = first + mm((scores[:half, :half] * top).astype(BF), part[:half], TN)
            first = first + mm((scores[half:, :half] * left).astype(BF), part[half:], TN)
            second = second + mm((scores[half:, half:] * right).astype(BF), part[half:], TN)
        blocks.append(jnp.concatenate([first, second], axis=0))
    d_stepped = jnp.concatenate(blocks, axis=1)
    d_top, d_left, d_right = d_top.astype(BF), d_left.astype(BF), d_right.astype(BF)
    d_shared_out[0, :half, :state] = mm(d_top, queries[:half], TN) + mm(d_left, queries[half:], TN)
    d_shared_out[0, half:, :state] = mm(d_right, queries[half:], TN)
    d_shared_out[0, :half, state:] = d_queries[:half] + mm(d_top, keys[:half])
    d_shared_out[0, half:, state:] = d_queries[half:] + mm(d_left, keys[:half]) + mm(d_right, keys[half:])
    skip = chan[1:2]
    d_values_out[0] = (skip * d_wide + step_wide * d_stepped).astype(BF)
    d_step = collapse(wide * d_stepped, size)
    d_rise = collapse(stepped.astype(F32) * d_stepped - d_wide * (full[0] - skip * wide), size)
    rates_out[0, :, :LANES] = d_rise
    rates_out[0, :, LANES:] = d_step


def state_back_body(
    channels, size, taps, info, lengths, feed, raw, rim, values, shared, rise, step, carried,
    d_values_in, d_shared_in, rates, conv_w, head_params, arrived, *rest
):
    d_pre_out, first_out, d_raw_out, conv_out, head_out, ext = rest
    seq = pl.program_id(0)
    after = get_state(arrived)
    length = feed.shape[1]
    state = shared.shape[2] // 2
    keys = shared[0, :, :state]
    wide = values[0].astype(F32)
    rise_all, step_all = rise[0], step[0]
    closing = rise_all[length - 1 :, :]
    ratio = jnp.exp(rise_all - closing)
    weight_wide = expand(ratio * step_all, channels, size)
    reached = mm(keys, after)
    d_values = d_values_in[0].astype(F32) + weight_wide * reached
    d_keys = d_shared_in[0, :, :state] + mm((weight_wide * wide).astype(BF), after, NT)
    d_queries = d_shared_in[0, :, state:]
    d_ratio = collapse(wide * reached, size) * ratio
    d_step = rates[0, :, LANES:] + d_ratio
    moved = d_ratio * step_all
    fade_terms = jnp.sum(after.astype(F32) * carried[0].astype(F32), axis=0, keepdims=True)
    d_fade = collapse(jnp.broadcast_to(fade_terms, (8, channels)), size)[0:1]
    d_close = jnp.sum(moved, axis=0, keepdims=True) + d_fade * jnp.exp(-closing)
    last = lax.broadcasted_iota(jnp.int32, (length, LANES), 0) == length - 1
    d_rise = rates[0, :, :LANES] + moved - jnp.where(last, d_close, 0.0)
    gathered = running_sum(d_rise, channels // size, True)
    params = head_params[...]
    rate = jnp.exp(params[1:2])
    valid = valid_column(info, lengths, seq, length)
    d_raw = (d_step + rate * gathered) * sigmoid(raw[0] + params[0:1]) * valid * params[2:3]
    d_raw_out[0] = d_raw.astype(BF)
    ext[:HALO] = rim[0]
    ext[HALO:] = feed[0]

    @pl.when(seq == 0)
    def _():
        conv_out[...] = jnp.zeros_like(conv_out)
        head_out[...] = jnp.zeros_like(head_out)

    head_out[0:1] += jnp.sum(d_raw, axis=0, keepdims=True)
    head_out[1:2] += rate * jnp.sum(step_all * gathered, axis=0, keepdims=True)
    for start, stop, d_act in (
        (0, channels, d_values),
        (channels, channels + state, d_keys),
        (channels + state, channels + 2 * state, d_queries),
    ):
        at = slice(start, stop)
        pre = conv_w[taps : taps + 1, at]
        for k in range(taps):
            begin = HALO - taps + 1 + k
            pre = pre + conv_w[k : k + 1, at] * ext[begin : begin + length, at]
        sig = sigmoid(pre)
        d_pre = d_act * valid * (sig * (1.0 + pre * (1.0 - sig)))
        d_pre_out[0, :, at] = d_pre
        first_out[0, :, at] = d_pre[:8]
        for k in range(taps):
            begin = HALO - taps + 1 + k
            conv_out[k : k + 1, at] += jnp.sum(d_pre * ext[begin : begin + length, at], axis=0, keepdims=True)
        conv_out[taps : taps + 1, at] += jnp.sum(d_pre, axis=0, keepdims=True)


def spread_body(n, nh, channels, taps, info, d_pre, d_next, d_gate, d_raw, w_z, w_x, w_bc, w_dt, conv_w, *refs):
    d_feed_out, outs, ext, table = refs[0], refs[1 : 1 + nh], refs[1 + nh], refs[2 + nh]
    length = d_pre.shape[1]
    ext[:length] = d_pre[0]
    ext[length:] = d_next[0]
    d_feed = conv_w[taps - 1 : taps] * ext[:length]
    for k in range(taps - 1):
        d_feed = d_feed + conv_w[k : k + 1] * ext[taps - 1 - k : taps - 1 - k + length]
    low = d_feed.astype(BF)
    d_feed_out[0] = low
    cols = w_z.shape[2]
    for s in range(n):
        at = slice(s * cols, (s + 1) * cols)
        running = mm(d_gate[0], w_z[s, 0], NT)
        running = running + mm(low[:, :channels], w_x[s, 0], NT)
        running = running + mm(low[:, channels:], w_bc[at, :], NT)
        table[:, at] = running + mm(d_raw[0], w_dt[:, at])
    scatter_rows(info, outs, table, length // nh)


def weight_body(groups, *refs):
    normal, grad, x, d_gate = (refs[i * groups : (i + 1) * groups] for i in range(4))
    out = refs[4 * groups]
    for place, (lefts, rights) in enumerate(((normal, grad), (x, d_gate))):
        summed = mm(lefts[0][...], rights[0][...], TN)
        for left, right in zip(lefts[1:], rights[1:]):
            summed = summed + mm(left[...], right[...], TN)
        out[0, place] = summed.astype(BF)


def feed_weight_body(nh, groups, channels, info, *refs):
    x, d_feed, d_raw = (refs[i * groups : (i + 1) * groups] for i in range(3))
    x_out, dt_out, *outs = refs[3 * groups : 3 * groups + 2 + nh]
    table = refs[3 * groups + 2 + nh]
    for g in range(groups):
        left = x[g][...]
        made = mm(left, d_feed[g][...], TN)
        steps = mm(d_raw[g][...], left, TN)[: dt_out.shape[1]]
        if g == 0:
            table[...] = made
            dt_out[0] = steps
        else:
            table[...] += made
            dt_out[0] += steps
    x_out[0] = table[:, :channels].astype(BF)
    own = table.shape[0] // nh
    for k, out in enumerate(outs):
        start = pl.multiple_of((info[0] ^ k) * own, own)
        out[0] = table[pl.ds(start, own), channels:].astype(BF)


def place_body(nh, info, *refs):
    pieces, out = refs[:nh], refs[nh]
    for k in range(nh):
        for layer in range(out.shape[0]):
            out[layer, info[0] ^ k] = pieces[k][layer].astype(F32)


def shards(
    hidden_in, grad_out, lengths, norm_gain, w_z, w_x, w_bc, w_dt, conv_x, conv_x_bias, conv_bc,
    conv_bc_bias, dt_bias, a_log, d_skip, y_gain, w_out,
):
    n, nh = lax.axis_size("seq"), lax.axis_size("heads")
    layers, depth, channels = w_z.shape
    width = depth * n
    heads_here = w_dt.shape[2]
    size = channels // heads_here
    both = w_bc.shape[2]
    state = both // 2
    taps = conv_x.shape[1]
    own, batches, _ = hidden_in.shape
    length = own * nh
    total = channels * nh
    feed_width = channels + both
    groups = GROUPS
    while batches % groups:
        groups //= 2
    part = batches // groups
    factor, per = max(1, n // part), max(1, part // n)
    narrow = channels // factor
    tokens = part * length
    here, place = lax.axis_index("heads"), lax.axis_index("seq")
    every = range(groups)
    infos = [jnp.stack([here, place, place * length, g * part]).astype(jnp.int32) for g in every]
    spans = [lengths[g * part : (g + 1) * part] for g in every]
    line = Line()
    call = line.call

    def flip(x, k):
        return lax.ppermute(x, "heads", [(i, i ^ k) for i in range(nh)])

    def along(x, s, keep=lambda i, j: True):
        pairs = [(i, (i + s) % n) for i in range(n) if keep(i, (i + s) % n)]
        return lax.ppermute(x, "seq", pairs)

    def gather_heads(x):
        evens = [x] + [flip(x, k) for k in range(2, nh, 2)]
        odds = [flip(piece, 1) for piece in evens]
        return [piece for pair in zip(evens, odds) for piece in pair]

    def scatter_heads(pieces):
        sums = [
            (pieces[k].astype(F32) + flip(pieces[k + 1], 1).astype(F32)).astype(BF)
            for k in range(0, nh, 2)
        ]
        return [sums[0]] + [flip(sums[k // 2], k) for k in range(2, nh, 2)]

    def gather_seq(x):
        return [x] + [along(x, s) for s in range(1, n)]

    def scatter_seq(a):
        own_part = lax.dynamic_index_in_dim(a, place, 0, False).astype(F32)
        for s in range(1, n):
            piece = lax.dynamic_index_in_dim(a, lax.rem(place + s, n), 0, False)
            own_part = own_part + along(piece, s).astype(F32)
        return own_part

    def in_order(parts):
        return jnp.roll(jnp.stack(parts[::-1]), place + 1, axis=0)

    rows_here = depth // nh
    share = lax.dynamic_slice_in_dim(w_bc, here * rows_here, rows_here, 1)
    step_rows = jnp.pad(w_dt.transpose(0, 2, 1), ((0, 0), (0, -heads_here % 16), (0, 0)))
    small = jnp.concatenate([share.reshape(-1, channels), step_rows.reshape(-1, channels)], axis=0)
    share_rows = share.size // channels
    weights = {}

    def fetch(*keys, after=None):
        sources = [{"x": w_x, "z": w_z, "o": w_out}[kind][layer] for kind, layer in keys]
        table = sources[0][None] if len(sources) == 1 else jnp.stack(sources)
        if not weights:
            table = jnp.concatenate([table, small.reshape(1, -1, channels)], axis=1)
        if after is not None:
            (table,) = line.hand_on([table], after)
        table = lax.all_gather(table, "seq", axis=0)
        for at, key in enumerate(keys):
            weights[key] = (table, at)

    fetch(("x", 0))
    fetch(("z", 0), ("o", 0))

    def weight_spec(table, at):
        return pl.BlockSpec((n, 1, depth, channels), lambda i: (0, at, 0, 0))

    gains = in_order(gather_seq(norm_gain)).transpose(1, 0, 2).reshape(layers, 1, width).astype(F32)
    x_res = [hidden_in[:, g * part : (g + 1) * part].transpose(1, 0, 2).astype(F32) for g in every]
    normed = []
    for g in every:
        outs = [sds((part, own, width), BF)]
        normed += call(
            first_norm_body, part, [x_res[g], gains[0]], [per_seq(x_res[g]), whole(gains[0])], outs,
            [per_seq(outs[0])], name="first_norm",
        )
    small = weights["x", 0][0][:, 0, depth:]
    shared_pieces = gather_heads(small[:, :share_rows].reshape(n, layers, rows_here, both))
    step_pieces = small[:, share_rows:].reshape(n, layers, -1, depth)
    collected = [sds((layers, n, nh, rows_here, both), BF), sds((layers, LANES, width), BF)]
    ins = [infos[0]] + shared_pieces + [step_pieces]
    shared_w, step_w = call(
        functools.partial(collect_body, n, nh), 1, ins, [smem()] + [whole(a) for a in ins[1:]],
        collected, [whole(a) for a in collected], name="collect",
    )
    shared_w = shared_w.reshape(layers, width, both)

    conv_all = jnp.concatenate([conv_x, conv_bc], axis=-1)
    bias_all = jnp.concatenate([conv_x_bias, conv_bc_bias], axis=-1)
    conv_all = jnp.concatenate(
        [conv_all, bias_all[:, None], jnp.zeros((layers, 7 - taps, feed_width), F32)], axis=1
    )
    lanes_used = (jnp.arange(LANES) < heads_here).astype(F32)
    pad_heads = lambda a: jnp.pad(a, ((0, 0), (0, LANES - heads_here)))
    head_all = jnp.stack(
        [pad_heads(dt_bias), pad_heads(a_log), jnp.broadcast_to(lanes_used, (layers, LANES))]
        + [jnp.zeros((layers, LANES), F32)] * 5,
        axis=1,
    )
    chan_all = jnp.stack(
        [y_gain, jnp.repeat(d_skip, size, axis=1)] + [jnp.zeros((layers, channels), F32)] * 6, axis=1
    )

    state_shape = sds((n, per, state, narrow), BF)
    state_spec = lambda rows: pl.BlockSpec((factor, 1, rows, narrow), lambda i: (i // per, i % per, 0, 0))

    def turn(states):
        return lax.all_to_all(states, "seq", 0, 0)

    def rim_of(pieces):
        rows = sum(
            jnp.where((here ^ k) == nh - 1, pieces[k][:, own - RIM :].astype(F32), 0.0) for k in range(nh)
        ).astype(BF)
        return along(rows.reshape(part * RIM, width), 1, lambda i, j: j == i + 1)

    stored = []
    for layer in range(layers):
        conv_w, head_params, chan = conv_all[layer], head_all[layer], chan_all[layer]
        wbc_full, wdt_full = shared_w[layer], step_w[layer]
        w_x_full, w_z_full, w_o_full = weights["x", layer], weights["z", layer], weights["o", layer]
        saved = [dict(x_res=x_res[g]) for g in every]
        arrived, states, local = [None] * groups, [None] * groups, [None] * groups
        for g in every:
            it = saved[g]
            pieces = gather_heads(normed[g])
            x_halo = rim_of(pieces)
            ins = [infos[g]] + pieces + [w_x_full[0], wbc_full, wdt_full]
            outs = [
                sds((part, length, width), BF),
                sds((part, length, feed_width), F32),
                sds((part, length, LANES), F32),
            ]
            it["x_all"], it["feed"], it["raw"] = call(
                functools.partial(project_body, nh, channels), part, ins,
                [smem()] + [per_seq(a) for a in pieces] + [weight_spec(*w_x_full), whole(wbc_full), whole(wdt_full)],
                outs, [per_seq(a) for a in outs],
                name="project",
            )
            ins = [infos[g], spans[g], it["feed"], it["raw"], x_halo, w_x_full[0], wbc_full, conv_w, head_params]
            outs = [
                sds((part, length, channels), BF),
                sds((part, length, both), BF),
                sds((part, length, LANES), F32),
                sds((part, length, LANES), F32),
                sds((n, per, state + FADES, narrow), BF),
                sds((part, HALO, feed_width), F32),
            ]
            specs = [per_seq(a) for a in outs]
            specs[4] = state_spec(state + FADES)
            it["values"], it["shared"], it["rise"], it["step"], states[g], it["rim"] = call(
                functools.partial(local_body, channels, size, taps), part, ins,
                [smem(), smem(), per_seq(ins[2]), per_seq(ins[3]), whole(x_halo), weight_spec(*w_x_full)]
                + [whole(a) for a in ins[6:]],
                outs, specs,
                scratch=[
                    pltpu.VMEM((HALO + length, feed_width), F32),
                    pltpu.VMEM((part, HALO, feed_width), F32),
                ],
                name="local",
            )
            arrived[g] = turn(states[g])
        for g in every:
            it = saved[g]
            ins = [it[k] for k in ("values", "shared", "rise", "step")] + [chan]
            outs = [sds((part, length, channels), F32)]
            (local[g],) = call(
                functools.partial(mix_body, size), part, ins, [per_seq(a) for a in ins[:-1]] + [whole(chan)],
                outs, [per_seq(outs[0])], name="mix",
            )

        def gate(g):
            it = saved[g]
            outs = [sds((part, length, channels), BF)]
            (it["gate"],) = call(
                gate_body, part, [it["x_all"], w_z_full[0]], [per_seq(it["x_all"]), weight_spec(*w_z_full)],
                outs, [per_seq(outs[0])], name="gate",
            )

        for g in every:
            outs = [state_shape, sds((n, per, 8, narrow), F32)]
            made, saved[g]["fades"] = call(
                chain_body, 1, [arrived[g]], [whole(arrived[g])], outs, [whole(a) for a in outs], name="chain"
            )
            arrived[g] = turn(made)
        for g in every:
            gate(g)
        if layer + 1 < layers:
            fetch(("x", layer + 1), ("z", layer + 1), after=arrived)
            fetch(("o", layer + 1), after=arrived)
        summed = [None] * groups
        for g in every:
            it = saved[g]
            ins = [infos[g], local[g], it["gate"], it["shared"], it["rise"], w_o_full[0], chan, arrived[g]]
            outs = [sds((part, length, channels), F32), sds((part, state, channels), BF)] + [
                sds((part, own, width + LANES), BF)
            ] * nh
            it["full"], it["carried"], *projected = call(
                functools.partial(output_body, n, nh, size), part, ins,
                [smem()] + [per_seq(a) for a in ins[1:5]] + [weight_spec(*w_o_full), whole(chan), state_spec(state)],
                outs, [per_seq(a) for a in outs],
                scratch=[pltpu.VMEM((length, width + LANES), F32)],
                name="output",
            )
            summed[g] = scatter_heads(projected)
        gain_next = gains[min(layer + 1, layers - 1)]
        for g in every:
            it = saved[g]
            ins = [infos[g], x_res[g], gain_next] + summed[g]
            outs = [
                sds((part, own, width), F32),
                sds((part, own, width), BF),
                sds((part, own, width), BF),
                sds((part, own, LANES), BF),
            ]
            x_res[g], it["branch"], normed[g], it["factor"] = call(
                functools.partial(norm_body, False, width, total), part, ins,
                [smem(), per_seq(ins[1]), whole(gain_next)] + [per_seq(a) for a in summed[g]],
                outs, [per_seq(a) for a in outs], name="norm",
            )
        stored.append(saved)

    grad_res, payload = [None] * groups, [None] * groups
    for g in every:
        top = stored[-1][g]
        grad_low = grad_out[:, g * part : (g + 1) * part].transpose(1, 0, 2)
        ins = [grad_low, top["branch"], top["factor"]]
        outs = [sds((part, own, width + LANES), BF)]
        (payload[g],) = call(
            first_back_body, part, ins, [per_seq(a) for a in ins], outs, [per_seq(a) for a in outs],
            name="first_back",
        )
        grad_res[g] = grad_low.astype(F32)
    flat = lambda a: a.reshape(tokens, a.shape[2])
    cut = pl.BlockSpec((tokens, depth), lambda i: (0, i))
    early_grads, late_grads = [None] * layers, [None] * layers

    def tied(layer, kernel):
        found = []
        for grads, (where, later) in ((early_grads, EARLY_AT), (late_grads, LATE_AT)):
            if where == kernel and 0 <= layer + later < layers and grads[layer + later] is not None:
                found.append(grads[layer + later])
        return found

    shared_grads, small_grads = [None] * layers, [None] * layers
    for layer in reversed(range(layers)):
        conv_w, head_params, chan = conv_all[layer], head_all[layer], chan_all[layer]
        wbc_full, wdt_full = shared_w[layer], step_w[layer]
        w_x_full, w_z_full, w_o_full = weights["x", layer], weights["z", layer], weights["o", layer]
        saved = stored[layer]
        work = [dict() for g in every]
        for g in every:
            it, to = saved[g], work[g]
            pieces = gather_heads(payload[g])
            ins = [infos[g]] + [it[k] for k in ("gate", "full", "values", "shared", "rise")]
            ins += [w_o_full[0], chan] + pieces
            outs = [
                sds((part, length, width), BF),
                sds((part, length, channels), BF),
                sds((part, length, channels), BF),
                sds((part, length, channels), BF),
                state_shape,
                sds((8, channels), F32),
            ]
            specs = [per_seq(a) for a in outs[:4]] + [state_spec(state), whole(outs[5])]
            to["grad"], to["d_gate"], to["normal"], to["d_full"], states[g], to["chan"] = call(
                functools.partial(gate_back_body, n, nh, size, total), part, ins,
                [smem()] + [per_seq(a) for a in ins[1:6]] + [weight_spec(*w_o_full), whole(chan)]
                + [per_seq(a) for a in pieces],
                outs, specs, scratch=[pltpu.VMEM((length, LANES), F32)],
                name="gate_back", after=tied(layer, "gate_back"),
            )
            arrived[g] = turn(states[g])
        def early_weights():
            ins = [flat(to["normal"]) for to in work] + [flat(to["grad"]) for to in work]
            ins += [flat(it["x_all"]) for it in saved] + [flat(to["d_gate"]) for to in work]
            outs = [sds((n, 2, depth, channels), BF)]
            (early,) = call(
                functools.partial(weight_body, groups), n, ins,
                [whole(a) for a in ins[:groups]] + [cut] * (2 * groups) + [whole(a) for a in ins[3 * groups :]],
                outs, [per_seq(outs[0])], name="early_weights",
            )
            return early

        def send_early(early, after=()):
            (held,) = line.hand_on([early], after)
            early_grads[layer] = lax.psum_scatter(held, "seq", scatter_dimension=0, tiled=False)

        def mix_back(g):
            it, to = saved[g], work[g]
            ins = [to["d_full"]] + [it[k] for k in ("full", "values", "shared", "rise", "step", "carried")] + [chan]
            outs = [
                sds((part, length, channels), BF),
                sds((part, length, both), F32),
                sds((part, length, 2 * LANES), F32),
            ]
            to["d_values"], to["d_shared"], to["d_rates"] = call(
                functools.partial(mix_back_body, size), part, ins,
                [per_seq(a) for a in ins[:-1]] + [whole(chan)], outs, [per_seq(a) for a in outs],
                name="mix_back", after=tied(layer, "mix_back"),
            )

        def state_back(g):
            it, to = saved[g], work[g]
            ins = [infos[g], spans[g]]
            ins += [it[k] for k in ("feed", "raw", "rim", "values", "shared", "rise", "step", "carried")]
            ins += [to["d_values"], to["d_shared"], to["d_rates"], conv_w, head_params, arrived[g]]
            outs = [
                sds((part, length, feed_width), F32),
                sds((part, 8, feed_width), F32),
                sds((part, length, LANES), BF),
                sds((8, feed_width), F32),
                sds((8, LANES), F32),
            ]
            to["d_pre"], first_rows, to["d_raw"], to["conv"], to["head"] = call(
                functools.partial(state_back_body, channels, size, taps), part, ins,
                [smem(), smem()] + [per_seq(a) for a in ins[2:13]] + [whole(conv_w), whole(head_params), state_spec(state)],
                outs, [per_seq(a) for a in outs[:3]] + [whole(a) for a in outs[3:]],
                scratch=[pltpu.VMEM((HALO + length, feed_width), F32)],
                name="state_back", after=tied(layer, "state_back"),
            )
            to["next"] = along(first_rows, -1, lambda i, j: j == i - 1)

        def spread(g):
            to = work[g]
            ins = [infos[g], to["d_pre"], to["next"], to["d_gate"], to["d_raw"]]
            ins += [w_z_full[0], w_x_full[0], wbc_full, wdt_full, conv_w]
            outs = [sds((part, length, feed_width), BF)] + [sds((part, own, width), BF)] * nh
            to["d_feed"], *pieces = call(
                functools.partial(spread_body, n, nh, channels, taps), part, ins,
                [smem()] + [per_seq(a) for a in ins[1:5]] + [weight_spec(*w_z_full), weight_spec(*w_x_full)]
                + [whole(a) for a in ins[7:]],
                outs, [per_seq(a) for a in outs],
                scratch=[pltpu.VMEM((length + 8, feed_width), F32), pltpu.VMEM((length, width), F32)],
                name="spread", after=tied(layer, "spread"),
            )
            to["summed"] = scatter_heads(pieces)

        early = early_weights()
        for g in every:
            fades = saved[g]["fades"]
            (made,) = call(
                chain_back_body, 1, [arrived[g], fades], [whole(arrived[g]), whole(fades)], [state_shape],
                [whole(state_shape)], name="chain_back",
            )
            arrived[g] = turn(made)
        for g in every:
            mix_back(g)
        send_early(early, arrived)
        for g in every:
            state_back(g)
        for g in every:
            spread(g)
        def late_weights(after):
            ins = [infos[0]] + [flat(it["x_all"]) for it in saved]
            ins += [flat(to["d_feed"]) for to in work] + [flat(to["d_raw"]) for to in work]
            outs = [sds((n, depth, channels), BF), sds((n, 16, depth), F32)] + [sds((n, rows_here, both), BF)] * nh
            d_wx, d_wdt, *shared_parts = call(
                functools.partial(feed_weight_body, nh, groups, channels), n, ins,
                [smem()] + [cut] * groups + [whole(a) for a in ins[1 + groups :]], outs, [per_seq(a) for a in outs],
                scratch=[pltpu.VMEM((depth, feed_width), F32)],
                    name="late_weights", after=after,
            )
            shared_grads[layer] = (shared_parts, d_wdt)
            return d_wx

        def send_late(d_wx, after=()):
            (held,) = line.hand_on([d_wx], after)
            late_grads[layer] = lax.psum_scatter(held, "seq", scatter_dimension=0, tiled=False)

        d_wx = late_weights([])
        if layer == 0:
            stacked = [jnp.stack([parts[k] for parts, steps in shared_grads], axis=1) for k in range(nh)]
            in_plane = sum(a.astype(F32) for a in scatter_heads(stacked)).astype(BF)
            steps = jnp.stack([steps for parts, steps in shared_grads], axis=1).astype(BF)
            send_late(
                jnp.concatenate([d_wx] + [a.reshape(n, -1, channels) for a in (in_plane, steps)], axis=1),
                early_grads[:1],
            )
        below = stored[max(layer - 1, 0)]
        for g in every:
            it, to = saved[g], work[g]
            ins = [it["x_res"], gains[layer], grad_res[g], below[g]["branch"], below[g]["factor"]] + to["summed"]
            outs = [
                sds((part, own, width), F32),
                sds((part, own, width + LANES), BF),
                sds((part, 8, width), F32),
            ]
            grad_res[g], payload[g], to["gain"] = call(
                functools.partial(back_norm_body, width), part, ins,
                [per_seq(ins[0]), whole(ins[1])] + [per_seq(a) for a in ins[2:]],
                outs, [per_seq(a) for a in outs], name="back_norm", after=tied(layer, "back_norm"),
            )
        if layer > 0:
            send_late(d_wx)
        small_grads[layer] = tuple(sum(to[k] for to in work) for k in ("chan", "conv", "head")) + (
            sum(jnp.sum(to["gain"][:, 0], axis=0) for to in work),
        )

    def sum_seq(a):
        return sum(gather_seq(a)[1:], a)

    def sum_heads(a):
        for bit in range(nh.bit_length() - 1):
            a = a + flip(a, 1 << bit)
        return a

    per_head = jnp.stack(
        [
            jnp.concatenate(
                [
                    s[0][:2].reshape(-1),
                    s[1][: taps + 1, :channels].reshape(-1),
                    s[2][:2].reshape(-1),
                    s[1][: taps + 1, channels:].reshape(-1),
                    s[3],
                ]
            )
            for s in small_grads
        ]
    )
    per_head = sum_seq(per_head)
    cut_at = 2 * channels + (taps + 1) * channels + 2 * LANES
    everywhere = sum_heads(per_head[:, cut_at:])
    chan_total = per_head[:, : 2 * channels].reshape(layers, 2, channels)
    conv_total = per_head[:, 2 * channels : (taps + 3) * channels].reshape(layers, taps + 1, channels)
    head_total = per_head[:, (taps + 3) * channels : cut_at].reshape(layers, 2, LANES)
    conv_shared = everywhere[:, : (taps + 1) * both].reshape(layers, taps + 1, both)
    gain_grad = lax.dynamic_slice_in_dim(everywhere[:, (taps + 1) * both :], place * depth, depth, 1)
    summed = late_grads[0][depth:]
    late_grads[0] = late_grads[0][:depth]
    split_at = layers * rows_here * both // channels
    pieces = gather_heads(summed[:split_at].reshape(layers, rows_here, both))
    step_sums = summed[split_at:].reshape(layers, -1, depth).astype(F32)
    ins = [infos[0]] + pieces
    outs = [sds((layers, nh, rows_here, both), F32)]
    (table,) = call(
        functools.partial(place_body, nh), 1, ins, [smem()] + [whole(a) for a in pieces],
        outs, [whole(outs[0])], name="place",
    )
    shared_grad = table.reshape(layers, depth, both)
    dt_grad = step_sums[:, :heads_here].transpose(0, 2, 1)
    back = lambda parts: jnp.concatenate(parts, axis=0).transpose(1, 0, 2)
    return (
        back(x_res),
        back(grad_res),
        gain_grad,
        jnp.stack([e[1] for e in early_grads]).astype(F32),
        jnp.stack(late_grads).astype(F32),
        shared_grad,
        dt_grad,
        conv_total[:, :taps],
        conv_total[:, taps],
        conv_shared[:, :taps],
        conv_shared[:, taps],
        head_total[:, 0, :heads_here],
        head_total[:, 1, :heads_here],
        jnp.sum(chan_total[:, 1].reshape(layers, heads_here, size), axis=-1),
        chan_total[:, 0],
        jnp.stack([e[0] for e in early_grads]).astype(F32),
    )


def solution(mesh):
    rows = P(("seq", "heads"), None, None)
    placed = (
        rows, rows, P(), P(None, "seq"), P(None, "seq", "heads"), P(None, "seq", "heads"),
        P(None, "seq", None), P(None, "seq", "heads"), P(None, None, "heads"), P(None, "heads"), P(), P(),
        P(None, "heads"), P(None, "heads"), P(None, "heads"), P(None, "heads"), P(None, "heads", "seq"),
    )
    made = (
        rows, rows, P(None, "seq"), P(None, "seq", "heads"), P(None, "seq", "heads"),
        P(None, "seq", None), P(None, "seq", "heads"), P(None, None, "heads"), P(None, "heads"), P(), P(),
        P(None, "heads"), P(None, "heads"), P(None, "heads"), P(None, "heads"), P(None, "heads", "seq"),
    )
    return jax.shard_map(shards, mesh=mesh, in_specs=placed, out_specs=made, check_vma=False)
```

```python
import functools

import jax
import jax.numpy as jnp
from jax import lax
from jax.experimental import pallas as pl
from jax.experimental.pallas import tpu as pltpu
from jax.sharding import PartitionSpec as P

F32 = jnp.float32
BF = jnp.bfloat16
EPSILON = 1e-05
LANES = 128
HALO = 8
RIM = 4
FADES = 16
NN = ((1,), (0,))
NT = ((1,), (1,))
TN = ((0,), (0,))
GROUPS = 1
EARLY_AT = ("state_back", 1)
LATE_AT = ("spread", 1)
VMEM_BYTES = 56 * 1024 * 1024


def mm(a, b, dims=NN):
    return lax.dot_general(a, b, (dims, ((), ())), preferred_element_type=F32)


def smem():
    return pl.BlockSpec(memory_space=pltpu.SMEM)


def anywhere():
    return pl.BlockSpec(memory_space=pl.ANY)


def whole(a):
    rank = len(a.shape)
    return pl.BlockSpec(tuple(a.shape), lambda i: (0,) * rank)


def per_seq(a):
    rank = len(a.shape)
    return pl.BlockSpec((1,) + tuple(a.shape[1:]), lambda i: (i,) + (0,) * (rank - 1))


def sds(shape, dtype):
    return jax.ShapeDtypeStruct(shape, dtype)


class Line:
    def __init__(self):
        self.last = ()

    def hand_on(self, arrays, after=()):
        shapes = [sds(a.shape, a.dtype) for a in arrays]
        return self.call(
            lambda *refs: None, 1, arrays, [anywhere()] * len(arrays), shapes, [anywhere()] * len(arrays),
            name="hand_on", after=after, aliases={i: i for i in range(len(arrays))},
        )

    def call(self, body, grid, ins, in_specs, outs, out_specs, scratch=(), name=None, after=(), aliases={}):
        waits = tuple(self.last) + tuple(after)
        count, extra = len(ins), len(waits)
        made = len(outs)

        def kernel(*refs):
            body(*refs[:count], *refs[count + extra : count + extra + made], *refs[count + extra + made + 1 :])
            refs[count + extra + made][...] = jnp.zeros((8, LANES), F32)

        mark = sds((8, LANES), F32)
        *results, token = pl.pallas_call(
            kernel,
            grid=(grid,),
            in_specs=list(in_specs) + [anywhere()] * extra,
            out_specs=list(out_specs) + [whole(mark)],
            out_shape=list(outs) + [mark],
            scratch_shapes=list(scratch),
            compiler_params=pltpu.CompilerParams(vmem_limit_bytes=VMEM_BYTES),
            cost_estimate=pl.CostEstimate(flops=1, bytes_accessed=1, transcendentals=0),
            input_output_aliases=aliases,
            name=name,
        )(*ins, *waits)
        self.last = (token,)
        return results


def head_lanes(heads, width, parts):
    shape = (LANES, width)
    lane = lax.broadcasted_iota(jnp.int32, shape, 0)
    head = lax.broadcasted_iota(jnp.int32, shape, 1) // (width // heads)
    hit = lane == head
    for part in range(1, parts):
        hit = hit | (lane == head + part * heads)
    return hit.astype(F32).astype(BF)


def three_parts(per_head, heads):
    lane = lax.broadcasted_iota(jnp.int32, per_head.shape, 1)
    x = jnp.where(lane < heads, per_head, 0.0)
    high = x.astype(BF).astype(F32)
    rest = x - high
    middle = rest.astype(BF).astype(F32)
    packed = high + pltpu.roll(middle, heads, 1) + pltpu.roll(rest - middle, 2 * heads, 1)
    return packed.astype(BF)


def expand(per_head, width, size):
    heads = width // size
    return mm(three_parts(per_head, heads), head_lanes(heads, width, 3))


def collapse(wide, size):
    width = wide.shape[1]
    heads = width // size
    high = wide.astype(BF)
    low = (wide - high.astype(F32)).astype(BF)
    shape = (width, LANES)
    table = lax.broadcasted_iota(jnp.int32, shape, 0) // size == lax.broadcasted_iota(jnp.int32, shape, 1)
    table = table.astype(F32).astype(BF)
    return mm(high, table) + mm(low, table)


def running_sum(per_head, heads, back=False):
    made = mm(triangle(per_head.shape[0], back).astype(BF), three_parts(per_head, heads))
    made = made + pltpu.roll(made, LANES - heads, 1) + pltpu.roll(made, LANES - 2 * heads, 1)
    lane = lax.broadcasted_iota(jnp.int32, made.shape, 1)
    return jnp.where(lane < heads, made, 0.0)


def sigmoid(x):
    return 0.5 * jnp.tanh(0.5 * x) + 0.5


def softplus(x):
    return jnp.maximum(x, 0.0) + jnp.log1p(jnp.exp(-jnp.abs(x)))


def valid_column(info, lengths, seq, length):
    rows = lax.broadcasted_iota(jnp.int32, (length, 1), 0) + info[2]
    return (rows < lengths[seq]).astype(F32)


def triangle(length, flipped=False):
    a = lax.broadcasted_iota(jnp.int32, (length, length), 0)
    b = lax.broadcasted_iota(jnp.int32, (length, length), 1)
    return ((a <= b) if flipped else (a >= b)).astype(F32)


def split_two(x):
    high = x.astype(BF)
    return high, (x - high.astype(F32)).astype(BF)


def lane_pack(columns, rows):
    lane = lax.broadcasted_iota(jnp.int32, (rows, LANES), 1)
    out = jnp.zeros((rows, LANES), F32)
    for place, column in enumerate(columns):
        out = jnp.where(lane == place, column.astype(F32), out)
    return out.astype(BF)


def decay_blocks(rise, rise_rows, head, length):
    half = length // 2
    column = rise[:, head : head + 1]
    row = rise_rows[head : head + 1, :]
    low = lax.broadcasted_iota(jnp.int32, (half, half), 0) >= lax.broadcasted_iota(
        jnp.int32, (half, half), 1
    )
    top = jnp.where(low, jnp.exp(row[:, :half] - column[:half]), 0.0)
    left = jnp.exp(row[:, :half] - column[half:])
    right = jnp.where(low, jnp.exp(row[:, half:] - column[half:]), 0.0)
    return top, left, right


def norm_body(last, width, total, info, x, gain, *refs):
    pieces, (x_out, branch_out, normed_out, payload_out) = refs[:-4], refs[-4:]
    summed = pieces[0][0].astype(F32)
    for piece in pieces[1:]:
        summed = summed + piece[0].astype(F32)
    squares = summed[:, width : width + 1] + summed[:, width + 1 : width + 2]
    factor = lax.rsqrt(squares / total + EPSILON)
    branch = summed[:, :width] * factor
    x_new = x[0] + branch
    x_out[0] = x_new
    branch_out[0] = branch.astype(BF)
    q = lax.rsqrt(jnp.mean(x_new * x_new, axis=-1, keepdims=True) + EPSILON)
    normed_out[0] = (x_new * q * gain[...]).astype(BF)
    high, low = split_two(factor)
    payload_out[0] = lane_pack((high, low), summed.shape[0])


def first_norm_body(x, gain, normed_out):
    x_new = x[0]
    q = lax.rsqrt(jnp.mean(x_new * x_new, axis=-1, keepdims=True) + EPSILON)
    normed_out[0] = (x_new * q * gain[...]).astype(BF)


def back_payload(grad_low, branch, factor_lanes, out):
    width = grad_low.shape[1]
    dotted = jnp.sum(grad_low.astype(F32) * branch.astype(F32), axis=-1, keepdims=True)
    high, low = split_two(dotted)
    lane = lax.broadcasted_iota(jnp.int32, (grad_low.shape[0], LANES), 1)
    lanes = factor_lanes.astype(F32)
    lanes = jnp.where(lane == 2, high.astype(F32), lanes)
    lanes = jnp.where(lane == 3, low.astype(F32), lanes)
    out[0, :, :width] = grad_low
    out[0, :, width:] = lanes.astype(BF)


def first_back_body(grad, branch, factor_lanes, out):
    back_payload(grad[0], branch[0], factor_lanes[0], out)


def back_norm_body(width, x, gain, grad, branch, factor_lanes, *refs):
    pieces, (grad_out, payload_out, gain_out) = refs[:-3], refs[-3:]
    d_normed = pieces[0][0].astype(F32)
    for piece in pieces[1:]:
        d_normed = d_normed + piece[0].astype(F32)
    rows = x[0]
    q = lax.rsqrt(jnp.mean(rows * rows, axis=-1, keepdims=True) + EPSILON)
    scaled = d_normed * gain[...]
    cross = jnp.sum(scaled * rows, axis=-1, keepdims=True)
    grad_new = grad[0] + q * scaled - rows * (q * q * q * cross / width)
    grad_out[0] = grad_new
    gain_out[0] = jnp.broadcast_to(
        jnp.sum(d_normed * rows * q, axis=0, keepdims=True), gain_out.shape[1:]
    )
    back_payload(grad_new.astype(BF), branch[0], factor_lanes[0], payload_out)


def collect_body(n, nh, info, *refs):
    pieces, steps = refs[:nh], refs[nh]
    shared_out, step_out = refs[nh + 1 :]
    step_out[...] = jnp.zeros_like(step_out)
    rows, wide = steps.shape[2:]
    for k in range(nh):
        for s in range(n):
            for layer in range(shared_out.shape[0]):
                shared_out[layer, s, info[0] ^ k] = pieces[k][s, layer]
    for s in range(n):
        for layer in range(step_out.shape[0]):
            step_out[layer, 0:rows, s * wide : (s + 1) * wide] = steps[s, layer]


def project_body(nh, channels, info, *refs):
    pieces = refs[:nh]
    w_x, w_bc, w_dt = refs[nh : nh + 3]
    x_out, feed_out, raw_out = refs[nh + 3 :]
    own = pieces[0].shape[1]
    for k in range(nh):
        start = pl.multiple_of((info[0] ^ k) * own, own)
        x_out[0, pl.ds(start, own), :] = pieces[k][0]
    rows = x_out[0]
    feed_out[0, :, :channels] = mm(rows, flat_rows(w_x))
    feed_out[0, :, channels:] = mm(rows, w_bc[...])
    raw_out[0] = mm(rows, w_dt[...], NT)


def flat_rows(w):
    table = w[...]
    return table.reshape(table.shape[0] * table.shape[2], table.shape[3])


def gate_body(x, w_z, gate_out):
    gate_out[0] = mm(x[0], flat_rows(w_z)).astype(BF)


def rates_of(raw, head_params):
    lanes = head_params[2:3]
    return softplus(raw + head_params[0:1]) * lanes


def local_body(
    channels, size, taps, info, lengths, feed, raw, x_halo, w_x, w_bc, conv_w, head_params,
    values_out, shared_out, rise_out, step_out, state_out, halo_out, ext, halo_all,
):
    seq = pl.program_id(0)
    length = feed.shape[1]
    state = (feed.shape[2] - channels) // 2

    @pl.when(seq == 0)
    def _():
        wide = mm(x_halo[...], flat_rows(w_x))
        narrow = mm(x_halo[...], w_bc[...])
        for m in range(halo_all.shape[0]):
            rows = slice(m * RIM, (m + 1) * RIM)
            halo_all[m, HALO - RIM :, :channels] = wide[rows]
            halo_all[m, HALO - RIM :, channels:] = narrow[rows]

    rim = halo_all[seq]
    halo_out[0] = rim
    ext[:HALO] = rim
    ext[HALO:] = feed[0]
    valid = valid_column(info, lengths, seq, length)
    pre = conv_w[taps : taps + 1]
    for k in range(taps):
        pre = pre + conv_w[k : k + 1] * ext[HALO - taps + 1 + k : HALO - taps + 1 + k + length]
    act = pre * sigmoid(pre) * valid
    low = act.astype(BF)
    values_out[0] = low[:, :channels]
    shared_out[0] = low[:, channels:]
    values = low[:, :channels].astype(F32)
    keys = low[:, channels : channels + state]
    params = head_params[...]
    step = rates_of(raw[0], params) * valid
    rise = running_sum(jnp.exp(params[1:2]) * step, channels // size)
    rise_out[0] = rise
    step_out[0] = step
    closing = rise[length - 1 :, :]
    weight = jnp.exp(rise - closing) * step
    weighted = (expand(weight, channels, size) * values).astype(BF)
    fade = expand(jnp.broadcast_to(jnp.exp(-closing), (FADES, LANES)), channels, size)
    put_state(state_out, mm(keys, weighted, TN), fade)


def mix_body(size, values, shared, rise_in, step, chan, local_out):
    length, channels = values.shape[1:]
    state = shared.shape[2] // 2
    keys, queries = shared[0, :, :state], shared[0, :, state:]
    wide = values[0].astype(F32)
    rise = rise_in[0]
    scores = mm(queries, keys, NT)
    stepped = (wide * expand(step[0], channels, size)).astype(BF)
    rise_rows = jnp.transpose(rise)
    half = length // 2
    group = LANES // size
    lane = lax.broadcasted_iota(jnp.int32, (length, LANES), 1) // size
    for pair in range(channels // LANES):
        block = stepped[:, pair * LANES : (pair + 1) * LANES]
        upper = jnp.zeros((half, LANES), F32)
        lower = jnp.zeros((half, LANES), F32)
        for inner in range(group):
            top, left, right = decay_blocks(rise, rise_rows, pair * group + inner, length)
            part = jnp.where(lane == inner, block, jnp.zeros_like(block))
            upper = upper + mm((scores[:half, :half] * top).astype(BF), part[:half])
            lower = lower + mm((scores[half:, :half] * left).astype(BF), part[:half])
            lower = lower + mm((scores[half:, half:] * right).astype(BF), part[half:])
        at = slice(pair * LANES, (pair + 1) * LANES)
        skipped = chan[1:2, at] * wide[:, at]
        local_out[0, :half, at] = upper + skipped[:half]
        local_out[0, half:, at] = lower + skipped[half:]


def put_state(out, made, fade=None):
    state, narrow = made.shape[0], out.shape[3]
    if fade is not None:
        high, low = split_two(fade)
        odd = lax.broadcasted_iota(jnp.int32, fade.shape, 0) % 2
        fade = jnp.where(odd == 0, high.astype(F32), low.astype(F32)).astype(BF)
    for j in range(out.shape[0]):
        at = slice(j * narrow, (j + 1) * narrow)
        out[j, 0, :state] = made[:, at].astype(BF)
        if fade is not None:
            out[j, 0, state:] = fade[:, at]


def get_state(part):
    pieces = [part[j, 0] for j in range(part.shape[0])]
    return pieces[0] if len(pieces) == 1 else jnp.concatenate(pieces, axis=1)


def chain_body(parts, carried, fades):
    state = carried.shape[2]
    for item in range(parts.shape[1]):
        running = jnp.zeros(carried.shape[2:], F32)
        for block in range(parts.shape[0]):
            carried[block, item] = running.astype(BF)
            rows = parts[block, item, state:].astype(F32)
            fade = rows[0:1] + rows[1:2]
            fades[block, item] = jnp.broadcast_to(fade, fades.shape[2:])
            running = fade * running + parts[block, item, :state].astype(F32)


def chain_back_body(parts, fades, carried):
    for item in range(parts.shape[1]):
        running = jnp.zeros(carried.shape[2:], F32)
        for block in range(parts.shape[0] - 1, -1, -1):
            carried[block, item] = running.astype(BF)
            running = fades[block, item, 0:1] * running + parts[block, item].astype(F32)


def scatter_rows(info, outs, table, own):
    for k, out in enumerate(outs):
        start = pl.multiple_of((info[0] ^ k) * own, own)
        out[0] = table[pl.ds(start, own), :].astype(BF)


def output_body(
    n, nh, size, info, local, gate, shared, rise, w_out, chan, arrived, *rest
):
    full_out, carried_out = rest[:2]
    outs, table = rest[2 : 2 + nh], rest[2 + nh]
    carried = get_state(arrived)
    carried_out[0] = carried
    length, channels = local.shape[1:]
    state = shared.shape[2] // 2
    queries = shared[0, :, state:]
    far = mm(queries, carried) * expand(jnp.exp(-rise[0]), channels, size)
    full = local[0] + far
    full_out[0] = full
    wide = gate[0].astype(F32)
    gated = full * wide * sigmoid(wide)
    squares = jnp.sum(gated * gated, axis=-1, keepdims=True)
    low = (gated * chan[0:1]).astype(BF)
    cols = w_out.shape[3]
    for s in range(n):
        table[:, s * cols : (s + 1) * cols] = mm(low, w_out[s, 0])
    high, rest_part = split_two(squares)
    table[:, n * cols :] = lane_pack((high, rest_part), length).astype(F32)
    scatter_rows(info, outs, table, length // nh)


def gate_back_body(
    n, nh, size, total, info, gate, full, values, shared, rise, w_out, chan, *refs
):
    pieces = refs[:nh]
    grad_out, d_gate_out, normal_out, d_full_out, state_out, sums_out, table = refs[nh:]
    seq = pl.program_id(0)
    own = pieces[0].shape[1]
    width = grad_out.shape[2]
    length, channels = gate.shape[1:]
    for k in range(nh):
        start = pl.multiple_of((info[0] ^ k) * own, own)
        grad_out[0, pl.ds(start, own), :] = pieces[k][0, :, :width]
        table[pl.ds(start, own), :] = pieces[k][0, :, width:].astype(F32)
    factor = table[:, 0:1] + table[:, 1:2]
    dotted = table[:, 2:3] + table[:, 3:4]
    cols = w_out.shape[3]
    d_normal = mm(grad_out[0, :, :cols], w_out[0, 0], NT)
    for s in range(1, n):
        d_normal = d_normal + mm(grad_out[0, :, s * cols : (s + 1) * cols], w_out[s, 0], NT)
    wide = gate[0].astype(F32)
    sig = sigmoid(wide)
    silu = wide * sig
    full_wide = full[0]
    gated = full_wide * silu
    gain = chan[0:1]
    normal = gated * factor
    normal_out[0] = (normal * gain).astype(BF)
    d_gated = factor * (d_normal * gain) - gated * (factor * factor * dotted / total)
    d_full = d_gated * silu
    d_gate_out[0] = (d_gated * full_wide * (sig * (1.0 + wide * (1.0 - sig)))).astype(BF)
    d_full_out[0] = d_full.astype(BF)
    state = shared.shape[2] // 2
    queries = shared[0, :, state:]
    spread = (d_full * expand(jnp.exp(-rise[0]), channels, size)).astype(BF)
    put_state(state_out, mm(queries, spread, TN))

    @pl.when(seq == 0)
    def _():
        sums_out[...] = jnp.zeros_like(sums_out)

    sums_out[0:1] += jnp.sum(d_normal * normal, axis=0, keepdims=True)
    sums_out[1:2] += jnp.sum(d_full * values[0].astype(F32), axis=0, keepdims=True)


def mix_back_body(
    size, d_full, full, values, shared, rise, step, carried, chan, d_values_out, d_shared_out, rates_out
):
    length, channels = d_full.shape[1:]
    state = shared.shape[2] // 2
    keys, queries = shared[0, :, :state], shared[0, :, state:]
    d_low = d_full[0]
    d_wide = d_low.astype(F32)
    wide = values[0].astype(F32)
    rise_all, step_all = rise[0], step[0]
    spread = (d_wide * expand(jnp.exp(-rise_all), channels, size)).astype(BF)
    d_queries = mm(spread, carried[0], NT)
    step_wide = expand(step_all, channels, size)
    stepped = (wide * step_wide).astype(BF)
    scores = mm(queries, keys, NT)
    rise_rows = jnp.transpose(rise_all)
    half = length // 2
    group = LANES // size
    lane = lax.broadcasted_iota(jnp.int32, (length, LANES), 1) // size
    d_top = jnp.zeros((half, half), F32)
    d_left = jnp.zeros((half, half), F32)
    d_right = jnp.zeros((half, half), F32)
    blocks = []
    for pair in range(channels // LANES):
        at = slice(pair * LANES, (pair + 1) * LANES)
        block, d_block = stepped[:, at], d_low[:, at]
        first = jnp.zeros((half, LANES), F32)
        second = jnp.zeros((half, LANES), F32)
        for inner in range(group):
            top, left, right = decay_blocks(rise_all, rise_rows, pair * group + inner, length)
            part = jnp.where(lane == inner, d_block, jnp.zeros_like(d_block))
            d_top = d_top + mm(part[:half], block[:half], NT) * top
            d_left = d_left + mm(part[half:], block[:half], NT) * left
            d_right = d_right + mm(part[half:], block[half:], NT) * right
            first = first + mm((scores[:half, :half] * top).astype(BF), part[:half], TN)
            first = first + mm((scores[half:, :half] * left).astype(BF), part[half:], TN)
            second = second + mm((scores[half:, half:] * right).astype(BF), part[half:], TN)
        blocks.append(jnp.concatenate([first, second], axis=0))
    d_stepped = jnp.concatenate(blocks, axis=1)
    d_top, d_left, d_right = d_top.astype(BF), d_left.astype(BF), d_right.astype(BF)
    d_shared_out[0, :half, :state] = mm(d_top, queries[:half], TN) + mm(d_left, queries[half:], TN)
    d_shared_out[0, half:, :state] = mm(d_right, queries[half:], TN)
    d_shared_out[0, :half, state:] = d_queries[:half] + mm(d_top, keys[:half])
    d_shared_out[0, half:, state:] = d_queries[half:] + mm(d_left, keys[:half]) + mm(d_right, keys[half:])
    skip = chan[1:2]
    d_values_out[0] = (skip * d_wide + step_wide * d_stepped).astype(BF)
    d_step = collapse(wide * d_stepped, size)
    d_rise = collapse(stepped.astype(F32) * d_stepped - d_wide * (full[0] - skip * wide), size)
    rates_out[0, :, :LANES] = d_rise
    rates_out[0, :, LANES:] = d_step


def state_back_body(
    channels, size, taps, info, lengths, feed, raw, rim, values, shared, rise, step, carried,
    d_values_in, d_shared_in, rates, conv_w, head_params, arrived, *rest
):
    d_pre_out, first_out, d_raw_out, conv_out, head_out, ext = rest
    seq = pl.program_id(0)
    after = get_state(arrived)
    length = feed.shape[1]
    state = shared.shape[2] // 2
    keys = shared[0, :, :state]
    wide = values[0].astype(F32)
    rise_all, step_all = rise[0], step[0]
    closing = rise_all[length - 1 :, :]
    ratio = jnp.exp(rise_all - closing)
    weight_wide = expand(ratio * step_all, channels, size)
    reached = mm(keys, after)
    d_values = d_values_in[0].astype(F32) + weight_wide * reached
    d_keys = d_shared_in[0, :, :state] + mm((weight_wide * wide).astype(BF), after, NT)
    d_queries = d_shared_in[0, :, state:]
    d_ratio = collapse(wide * reached, size) * ratio
    d_step = rates[0, :, LANES:] + d_ratio
    moved = d_ratio * step_all
    fade_terms = jnp.sum(after.astype(F32) * carried[0].astype(F32), axis=0, keepdims=True)
    d_fade = collapse(jnp.broadcast_to(fade_terms, (8, channels)), size)[0:1]
    d_close = jnp.sum(moved, axis=0, keepdims=True) + d_fade * jnp.exp(-closing)
    last = lax.broadcasted_iota(jnp.int32, (length, LANES), 0) == length - 1
    d_rise = rates[0, :, :LANES] + moved - jnp.where(last, d_close, 0.0)
    gathered = running_sum(d_rise, channels // size, True)
    params = head_params[...]
    rate = jnp.exp(params[1:2])
    valid = valid_column(info, lengths, seq, length)
    d_raw = (d_step + rate * gathered) * sigmoid(raw[0] + params[0:1]) * valid * params[2:3]
    d_raw_out[0] = d_raw.astype(BF)
    ext[:HALO] = rim[0]
    ext[HALO:] = feed[0]

    @pl.when(seq == 0)
    def _():
        conv_out[...] = jnp.zeros_like(conv_out)
        head_out[...] = jnp.zeros_like(head_out)

    head_out[0:1] += jnp.sum(d_raw, axis=0, keepdims=True)
    head_out[1:2] += rate * jnp.sum(step_all * gathered, axis=0, keepdims=True)
    for start, stop, d_act in (
        (0, channels, d_values),
        (channels, channels + state, d_keys),
        (channels + state, channels + 2 * state, d_queries),
    ):
        at = slice(start, stop)
        pre = conv_w[taps : taps + 1, at]
        for k in range(taps):
            begin = HALO - taps + 1 + k
            pre = pre + conv_w[k : k + 1, at] * ext[begin : begin + length, at]
        sig = sigmoid(pre)
        d_pre = d_act * valid * (sig * (1.0 + pre * (1.0 - sig)))
        d_pre_out[0, :, at] = d_pre
        first_out[0, :, at] = d_pre[:8]
        for k in range(taps):
            begin = HALO - taps + 1 + k
            conv_out[k : k + 1, at] += jnp.sum(d_pre * ext[begin : begin + length, at], axis=0, keepdims=True)
        conv_out[taps : taps + 1, at] += jnp.sum(d_pre, axis=0, keepdims=True)


def spread_body(n, nh, channels, taps, info, d_pre, d_next, d_gate, d_raw, w_z, w_x, w_bc, w_dt, conv_w, *refs):
    d_feed_out, outs, ext, table = refs[0], refs[1 : 1 + nh], refs[1 + nh], refs[2 + nh]
    length = d_pre.shape[1]
    ext[:length] = d_pre[0]
    ext[length:] = d_next[0]
    d_feed = conv_w[taps - 1 : taps] * ext[:length]
    for k in range(taps - 1):
        d_feed = d_feed + conv_w[k : k + 1] * ext[taps - 1 - k : taps - 1 - k + length]
    low = d_feed.astype(BF)
    d_feed_out[0] = low
    cols = w_z.shape[2]
    for s in range(n):
        at = slice(s * cols, (s + 1) * cols)
        running = mm(d_gate[0], w_z[s, 0], NT)
        running = running + mm(low[:, :channels], w_x[s, 0], NT)
        running = running + mm(low[:, channels:], w_bc[at, :], NT)
        table[:, at] = running + mm(d_raw[0], w_dt[:, at])
    scatter_rows(info, outs, table, length // nh)


def weight_body(groups, *refs):
    normal, grad, x, d_gate = (refs[i * groups : (i + 1) * groups] for i in range(4))
    out = refs[4 * groups]
    for place, (lefts, rights) in enumerate(((normal, grad), (x, d_gate))):
        summed = mm(lefts[0][...], rights[0][...], TN)
        for left, right in zip(lefts[1:], rights[1:]):
            summed = summed + mm(left[...], right[...], TN)
        out[0, place] = summed.astype(BF)


def feed_weight_body(nh, groups, channels, info, *refs):
    x, d_feed, d_raw = (refs[i * groups : (i + 1) * groups] for i in range(3))
    x_out, dt_out, *outs = refs[3 * groups : 3 * groups + 2 + nh]
    table = refs[3 * groups + 2 + nh]
    for g in range(groups):
        left = x[g][...]
        made = mm(left, d_feed[g][...], TN)
        steps = mm(d_raw[g][...], left, TN)[: dt_out.shape[1]]
        if g == 0:
            table[...] = made
            dt_out[0] = steps
        else:
            table[...] += made
            dt_out[0] += steps
    x_out[0] = table[:, :channels].astype(BF)
    own = table.shape[0] // nh
    for k, out in enumerate(outs):
        start = pl.multiple_of((info[0] ^ k) * own, own)
        out[0] = table[pl.ds(start, own), channels:].astype(BF)


def place_body(nh, info, *refs):
    pieces, out = refs[:nh], refs[nh]
    for k in range(nh):
        for layer in range(out.shape[0]):
            out[layer, info[0] ^ k] = pieces[k][layer].astype(F32)


def shards(
    hidden_in, grad_out, lengths, norm_gain, w_z, w_x, w_bc, w_dt, conv_x, conv_x_bias, conv_bc,
    conv_bc_bias, dt_bias, a_log, d_skip, y_gain, w_out,
):
    n, nh = lax.axis_size("seq"), lax.axis_size("heads")
    layers, depth, channels = w_z.shape
    width = depth * n
    heads_here = w_dt.shape[2]
    size = channels // heads_here
    both = w_bc.shape[2]
    state = both // 2
    taps = conv_x.shape[1]
    own, batches, _ = hidden_in.shape
    length = own * nh
    total = channels * nh
    feed_width = channels + both
    groups = GROUPS
    while batches % groups:
        groups //= 2
    part = batches // groups
    factor, per = max(1, n // part), max(1, part // n)
    narrow = channels // factor
    tokens = part * length
    here, place = lax.axis_index("heads"), lax.axis_index("seq")
    every = range(groups)
    infos = [jnp.stack([here, place, place * length, g * part]).astype(jnp.int32) for g in every]
    spans = [lengths[g * part : (g + 1) * part] for g in every]
    line = Line()
    call = line.call

    def flip(x, k):
        return lax.ppermute(x, "heads", [(i, i ^ k) for i in range(nh)])

    def along(x, s, keep=lambda i, j: True):
        pairs = [(i, (i + s) % n) for i in range(n) if keep(i, (i + s) % n)]
        return lax.ppermute(x, "seq", pairs)

    def gather_heads(x):
        evens = [x] + [flip(x, k) for k in range(2, nh, 2)]
        odds = [flip(piece, 1) for piece in evens]
        return [piece for pair in zip(evens, odds) for piece in pair]

    def scatter_heads(pieces):
        sums = [
            (pieces[k].astype(F32) + flip(pieces[k + 1], 1).astype(F32)).astype(BF)
            for k in range(0, nh, 2)
        ]
        return [sums[0]] + [flip(sums[k // 2], k) for k in range(2, nh, 2)]

    def gather_seq(x):
        return [x] + [along(x, s) for s in range(1, n)]

    def scatter_seq(a):
        own_part = lax.dynamic_index_in_dim(a, place, 0, False).astype(F32)
        for s in range(1, n):
            piece = lax.dynamic_index_in_dim(a, lax.rem(place + s, n), 0, False)
            own_part = own_part + along(piece, s).astype(F32)
        return own_part

    def in_order(parts):
        return jnp.roll(jnp.stack(parts[::-1]), place + 1, axis=0)

    rows_here = depth // nh
    share = lax.dynamic_slice_in_dim(w_bc, here * rows_here, rows_here, 1)
    step_rows = jnp.pad(w_dt.transpose(0, 2, 1), ((0, 0), (0, -heads_here % 16), (0, 0)))
    small = jnp.concatenate([share.reshape(-1, channels), step_rows.reshape(-1, channels)], axis=0)
    share_rows = share.size // channels
    weights = {}

    def fetch(*keys, after=None):
        sources = [{"x": w_x, "z": w_z, "o": w_out}[kind][layer] for kind, layer in keys]
        table = sources[0][None] if len(sources) == 1 else jnp.stack(sources)
        if after is not None:
            (table,) = line.hand_on([table], after)
        table = lax.all_gather(table, "seq", axis=0)
        for at, key in enumerate(keys):
            weights[key] = (table, at)

    fetch(("x", 0))
    fetch(("z", 0), ("o", 0))

    def weight_spec(table, at):
        return pl.BlockSpec((n, 1, depth, channels), lambda i: (0, at, 0, 0))

    gains = in_order(gather_seq(norm_gain)).transpose(1, 0, 2).reshape(layers, 1, width).astype(F32)
    x_res = [hidden_in[:, g * part : (g + 1) * part].transpose(1, 0, 2).astype(F32) for g in every]
    normed = []
    for g in every:
        outs = [sds((part, own, width), BF)]
        normed += call(
            first_norm_body, part, [x_res[g], gains[0]], [per_seq(x_res[g]), whole(gains[0])], outs,
            [per_seq(outs[0])], name="first_norm",
        )
    small = in_order(gather_seq(small))
    shared_pieces = gather_heads(small[:, :share_rows].reshape(n, layers, rows_here, both))
    step_pieces = small[:, share_rows:].reshape(n, layers, -1, depth)
    collected = [sds((layers, n, nh, rows_here, both), BF), sds((layers, LANES, width), BF)]
    ins = [infos[0]] + shared_pieces + [step_pieces]
    shared_w, step_w = call(
        functools.partial(collect_body, n, nh), 1, ins, [smem()] + [whole(a) for a in ins[1:]],
        collected, [whole(a) for a in collected], name="collect",
    )
    shared_w = shared_w.reshape(layers, width, both)

    conv_all = jnp.concatenate([conv_x, conv_bc], axis=-1)
    bias_all = jnp.concatenate([conv_x_bias, conv_bc_bias], axis=-1)
    conv_all = jnp.concatenate(
        [conv_all, bias_all[:, None], jnp.zeros((layers, 7 - taps, feed_width), F32)], axis=1
    )
    lanes_used = (jnp.arange(LANES) < heads_here).astype(F32)
    pad_heads = lambda a: jnp.pad(a, ((0, 0), (0, LANES - heads_here)))
    head_all = jnp.stack(
        [pad_heads(dt_bias), pad_heads(a_log), jnp.broadcast_to(lanes_used, (layers, LANES))]
        + [jnp.zeros((layers, LANES), F32)] * 5,
        axis=1,
    )
    chan_all = jnp.stack(
        [y_gain, jnp.repeat(d_skip, size, axis=1)] + [jnp.zeros((layers, channels), F32)] * 6, axis=1
    )

    state_shape = sds((n, per, state, narrow), BF)
    state_spec = lambda rows: pl.BlockSpec((factor, 1, rows, narrow), lambda i: (i // per, i % per, 0, 0))

    def turn(states):
        return lax.all_to_all(states, "seq", 0, 0)

    def rim_of(pieces):
        rows = sum(
            jnp.where((here ^ k) == nh - 1, pieces[k][:, own - RIM :].astype(F32), 0.0) for k in range(nh)
        ).astype(BF)
        return along(rows.reshape(part * RIM, width), 1, lambda i, j: j == i + 1)

    stored = []
    for layer in range(layers):
        conv_w, head_params, chan = conv_all[layer], head_all[layer], chan_all[layer]
        wbc_full, wdt_full = shared_w[layer], step_w[layer]
        w_x_full, w_z_full, w_o_full = weights["x", layer], weights["z", layer], weights["o", layer]
        saved = [dict(x_res=x_res[g]) for g in every]
        arrived, states, local = [None] * groups, [None] * groups, [None] * groups
        for g in every:
            it = saved[g]
            pieces = gather_heads(normed[g])
            x_halo = rim_of(pieces)
            ins = [infos[g]] + pieces + [w_x_full[0], wbc_full, wdt_full]
            outs = [
                sds((part, length, width), BF),
                sds((part, length, feed_width), F32),
                sds((part, length, LANES), F32),
            ]
            it["x_all"], it["feed"], it["raw"] = call(
                functools.partial(project_body, nh, channels), part, ins,
                [smem()] + [per_seq(a) for a in pieces] + [weight_spec(*w_x_full), whole(wbc_full), whole(wdt_full)],
                outs, [per_seq(a) for a in outs],
                name="project",
            )
            ins = [infos[g], spans[g], it["feed"], it["raw"], x_halo, w_x_full[0], wbc_full, conv_w, head_params]
            outs = [
                sds((part, length, channels), BF),
                sds((part, length, both), BF),
                sds((part, length, LANES), F32),
                sds((part, length, LANES), F32),
                sds((n, per, state + FADES, narrow), BF),
                sds((part, HALO, feed_width), F32),
            ]
            specs = [per_seq(a) for a in outs]
            specs[4] = state_spec(state + FADES)
            it["values"], it["shared"], it["rise"], it["step"], states[g], it["rim"] = call(
                functools.partial(local_body, channels, size, taps), part, ins,
                [smem(), smem(), per_seq(ins[2]), per_seq(ins[3]), whole(x_halo), weight_spec(*w_x_full)]
                + [whole(a) for a in ins[6:]],
                outs, specs,
                scratch=[
                    pltpu.VMEM((HALO + length, feed_width), F32),
                    pltpu.VMEM((part, HALO, feed_width), F32),
                ],
                name="local",
            )
            arrived[g] = turn(states[g])
        for g in every:
            it = saved[g]
            ins = [it[k] for k in ("values", "shared", "rise", "step")] + [chan]
            outs = [sds((part, length, channels), F32)]
            (local[g],) = call(
                functools.partial(mix_body, size), part, ins, [per_seq(a) for a in ins[:-1]] + [whole(chan)],
                outs, [per_seq(outs[0])], name="mix",
            )

        def gate(g):
            it = saved[g]
            outs = [sds((part, length, channels), BF)]
            (it["gate"],) = call(
                gate_body, part, [it["x_all"], w_z_full[0]], [per_seq(it["x_all"]), weight_spec(*w_z_full)],
                outs, [per_seq(outs[0])], name="gate",
            )

        for g in every:
            outs = [state_shape, sds((n, per, 8, narrow), F32)]
            made, saved[g]["fades"] = call(
                chain_body, 1, [arrived[g]], [whole(arrived[g])], outs, [whole(a) for a in outs], name="chain"
            )
            arrived[g] = turn(made)
        for g in every:
            gate(g)
        if layer + 1 < layers:
            fetch(("x", layer + 1), ("z", layer + 1), after=arrived)
            fetch(("o", layer + 1), after=arrived)
        summed = [None] * groups
        for g in every:
            it = saved[g]
            ins = [infos[g], local[g], it["gate"], it["shared"], it["rise"], w_o_full[0], chan, arrived[g]]
            outs = [sds((part, length, channels), F32), sds((part, state, channels), BF)] + [
                sds((part, own, width + LANES), BF)
            ] * nh
            it["full"], it["carried"], *projected = call(
                functools.partial(output_body, n, nh, size), part, ins,
                [smem()] + [per_seq(a) for a in ins[1:5]] + [weight_spec(*w_o_full), whole(chan), state_spec(state)],
                outs, [per_seq(a) for a in outs],
                scratch=[pltpu.VMEM((length, width + LANES), F32)],
                name="output",
            )
            summed[g] = scatter_heads(projected)
        gain_next = gains[min(layer + 1, layers - 1)]
        for g in every:
            it = saved[g]
            ins = [infos[g], x_res[g], gain_next] + summed[g]
            outs = [
                sds((part, own, width), F32),
                sds((part, own, width), BF),
                sds((part, own, width), BF),
                sds((part, own, LANES), BF),
            ]
            x_res[g], it["branch"], normed[g], it["factor"] = call(
                functools.partial(norm_body, False, width, total), part, ins,
                [smem(), per_seq(ins[1]), whole(gain_next)] + [per_seq(a) for a in summed[g]],
                outs, [per_seq(a) for a in outs], name="norm",
            )
        stored.append(saved)

    grad_res, payload = [None] * groups, [None] * groups
    for g in every:
        top = stored[-1][g]
        grad_low = grad_out[:, g * part : (g + 1) * part].transpose(1, 0, 2)
        ins = [grad_low, top["branch"], top["factor"]]
        outs = [sds((part, own, width + LANES), BF)]
        (payload[g],) = call(
            first_back_body, part, ins, [per_seq(a) for a in ins], outs, [per_seq(a) for a in outs],
            name="first_back",
        )
        grad_res[g] = grad_low.astype(F32)
    flat = lambda a: a.reshape(tokens, a.shape[2])
    cut = pl.BlockSpec((tokens, depth), lambda i: (0, i))
    early_grads, late_grads = [None] * layers, [None] * layers

    def tied(layer, kernel):
        found = []
        for grads, (where, later) in ((early_grads, EARLY_AT), (late_grads, LATE_AT)):
            if where == kernel and 0 <= layer + later < layers and grads[layer + later] is not None:
                found.append(grads[layer + later])
        return found

    shared_grads, small_grads = [None] * layers, [None] * layers
    for layer in reversed(range(layers)):
        conv_w, head_params, chan = conv_all[layer], head_all[layer], chan_all[layer]
        wbc_full, wdt_full = shared_w[layer], step_w[layer]
        w_x_full, w_z_full, w_o_full = weights["x", layer], weights["z", layer], weights["o", layer]
        saved = stored[layer]
        work = [dict() for g in every]
        for g in every:
            it, to = saved[g], work[g]
            pieces = gather_heads(payload[g])
            ins = [infos[g]] + [it[k] for k in ("gate", "full", "values", "shared", "rise")]
            ins += [w_o_full[0], chan] + pieces
            outs = [
                sds((part, length, width), BF),
                sds((part, length, channels), BF),
                sds((part, length, channels), BF),
                sds((part, length, channels), BF),
                state_shape,
                sds((8, channels), F32),
            ]
            specs = [per_seq(a) for a in outs[:4]] + [state_spec(state), whole(outs[5])]
            to["grad"], to["d_gate"], to["normal"], to["d_full"], states[g], to["chan"] = call(
                functools.partial(gate_back_body, n, nh, size, total), part, ins,
                [smem()] + [per_seq(a) for a in ins[1:6]] + [weight_spec(*w_o_full), whole(chan)]
                + [per_seq(a) for a in pieces],
                outs, specs, scratch=[pltpu.VMEM((length, LANES), F32)],
                name="gate_back", after=tied(layer, "gate_back"),
            )
            arrived[g] = turn(states[g])
        def early_weights():
            ins = [flat(to["normal"]) for to in work] + [flat(to["grad"]) for to in work]
            ins += [flat(it["x_all"]) for it in saved] + [flat(to["d_gate"]) for to in work]
            outs = [sds((n, 2, depth, channels), BF)]
            (early,) = call(
                functools.partial(weight_body, groups), n, ins,
                [whole(a) for a in ins[:groups]] + [cut] * (2 * groups) + [whole(a) for a in ins[3 * groups :]],
                outs, [per_seq(outs[0])], name="early_weights",
            )
            return early

        def send_early(early, after=()):
            (held,) = line.hand_on([early], after)
            early_grads[layer] = lax.psum_scatter(held, "seq", scatter_dimension=0, tiled=False)

        def mix_back(g):
            it, to = saved[g], work[g]
            ins = [to["d_full"]] + [it[k] for k in ("full", "values", "shared", "rise", "step", "carried")] + [chan]
            outs = [
                sds((part, length, channels), BF),
                sds((part, length, both), F32),
                sds((part, length, 2 * LANES), F32),
            ]
            to["d_values"], to["d_shared"], to["d_rates"] = call(
                functools.partial(mix_back_body, size), part, ins,
                [per_seq(a) for a in ins[:-1]] + [whole(chan)], outs, [per_seq(a) for a in outs],
                name="mix_back", after=tied(layer, "mix_back"),
            )

        def state_back(g):
            it, to = saved[g], work[g]
            ins = [infos[g], spans[g]]
            ins += [it[k] for k in ("feed", "raw", "rim", "values", "shared", "rise", "step", "carried")]
            ins += [to["d_values"], to["d_shared"], to["d_rates"], conv_w, head_params, arrived[g]]
            outs = [
                sds((part, length, feed_width), F32),
                sds((part, 8, feed_width), F32),
                sds((part, length, LANES), BF),
                sds((8, feed_width), F32),
                sds((8, LANES), F32),
            ]
            to["d_pre"], first_rows, to["d_raw"], to["conv"], to["head"] = call(
                functools.partial(state_back_body, channels, size, taps), part, ins,
                [smem(), smem()] + [per_seq(a) for a in ins[2:13]] + [whole(conv_w), whole(head_params), state_spec(state)],
                outs, [per_seq(a) for a in outs[:3]] + [whole(a) for a in outs[3:]],
                scratch=[pltpu.VMEM((HALO + length, feed_width), F32)],
                name="state_back", after=tied(layer, "state_back"),
            )
            to["next"] = along(first_rows, -1, lambda i, j: j == i - 1)

        def spread(g):
            to = work[g]
            ins = [infos[g], to["d_pre"], to["next"], to["d_gate"], to["d_raw"]]
            ins += [w_z_full[0], w_x_full[0], wbc_full, wdt_full, conv_w]
            outs = [sds((part, length, feed_width), BF)] + [sds((part, own, width), BF)] * nh
            to["d_feed"], *pieces = call(
                functools.partial(spread_body, n, nh, channels, taps), part, ins,
                [smem()] + [per_seq(a) for a in ins[1:5]] + [weight_spec(*w_z_full), weight_spec(*w_x_full)]
                + [whole(a) for a in ins[7:]],
                outs, [per_seq(a) for a in outs],
                scratch=[pltpu.VMEM((length + 8, feed_width), F32), pltpu.VMEM((length, width), F32)],
                name="spread", after=tied(layer, "spread"),
            )
            to["summed"] = scatter_heads(pieces)

        early = early_weights()
        for g in every:
            fades = saved[g]["fades"]
            (made,) = call(
                chain_back_body, 1, [arrived[g], fades], [whole(arrived[g]), whole(fades)], [state_shape],
                [whole(state_shape)], name="chain_back",
            )
            arrived[g] = turn(made)
        for g in every:
            mix_back(g)
        send_early(early, arrived)
        for g in every:
            state_back(g)
        for g in every:
            spread(g)
        def late_weights(after):
            ins = [infos[0]] + [flat(it["x_all"]) for it in saved]
            ins += [flat(to["d_feed"]) for to in work] + [flat(to["d_raw"]) for to in work]
            outs = [sds((n, depth, channels), BF), sds((n, 16, depth), F32)] + [sds((n, rows_here, both), BF)] * nh
            d_wx, d_wdt, *shared_parts = call(
                functools.partial(feed_weight_body, nh, groups, channels), n, ins,
                [smem()] + [cut] * groups + [whole(a) for a in ins[1 + groups :]], outs, [per_seq(a) for a in outs],
                scratch=[pltpu.VMEM((depth, feed_width), F32)],
                    name="late_weights", after=after,
            )
            shared_grads[layer] = (shared_parts, d_wdt)
            return d_wx

        def send_late(d_wx, after=()):
            (held,) = line.hand_on([d_wx], after)
            late_grads[layer] = lax.psum_scatter(held, "seq", scatter_dimension=0, tiled=False)

        d_wx = late_weights([])
        if layer == 0:
            stacked = [jnp.stack([parts[k] for parts, steps in shared_grads], axis=1) for k in range(nh)]
            in_plane = sum(a.astype(F32) for a in scatter_heads(stacked)).astype(BF)
            steps = jnp.stack([steps for parts, steps in shared_grads], axis=1).astype(BF)
            send_late(
                jnp.concatenate([d_wx] + [a.reshape(n, -1, channels) for a in (in_plane, steps)], axis=1),
                early_grads[:1],
            )
        below = stored[max(layer - 1, 0)]
        for g in every:
            it, to = saved[g], work[g]
            ins = [it["x_res"], gains[layer], grad_res[g], below[g]["branch"], below[g]["factor"]] + to["summed"]
            outs = [
                sds((part, own, width), F32),
                sds((part, own, width + LANES), BF),
                sds((part, 8, width), F32),
            ]
            grad_res[g], payload[g], to["gain"] = call(
                functools.partial(back_norm_body, width), part, ins,
                [per_seq(ins[0]), whole(ins[1])] + [per_seq(a) for a in ins[2:]],
                outs, [per_seq(a) for a in outs], name="back_norm", after=tied(layer, "back_norm"),
            )
        if layer > 0:
            send_late(d_wx)
        small_grads[layer] = tuple(sum(to[k] for to in work) for k in ("chan", "conv", "head")) + (
            sum(jnp.sum(to["gain"][:, 0], axis=0) for to in work),
        )

    def sum_seq(a):
        return sum(gather_seq(a)[1:], a)

    def sum_heads(a):
        for bit in range(nh.bit_length() - 1):
            a = a + flip(a, 1 << bit)
        return a

    per_head = jnp.stack(
        [
            jnp.concatenate(
                [
                    s[0][:2].reshape(-1),
                    s[1][: taps + 1, :channels].reshape(-1),
                    s[2][:2].reshape(-1),
                    s[1][: taps + 1, channels:].reshape(-1),
                    s[3],
                ]
            )
            for s in small_grads
        ]
    )
    per_head = sum_seq(per_head)
    cut_at = 2 * channels + (taps + 1) * channels + 2 * LANES
    everywhere = sum_heads(per_head[:, cut_at:])
    chan_total = per_head[:, : 2 * channels].reshape(layers, 2, channels)
    conv_total = per_head[:, 2 * channels : (taps + 3) * channels].reshape(layers, taps + 1, channels)
    head_total = per_head[:, (taps + 3) * channels : cut_at].reshape(layers, 2, LANES)
    conv_shared = everywhere[:, : (taps + 1) * both].reshape(layers, taps + 1, both)
    gain_grad = lax.dynamic_slice_in_dim(everywhere[:, (taps + 1) * both :], place * depth, depth, 1)
    summed = late_grads[0][depth:]
    late_grads[0] = late_grads[0][:depth]
    split_at = layers * rows_here * both // channels
    pieces = gather_heads(summed[:split_at].reshape(layers, rows_here, both))
    step_sums = summed[split_at:].reshape(layers, -1, depth).astype(F32)
    ins = [infos[0]] + pieces
    outs = [sds((layers, nh, rows_here, both), F32)]
    (table,) = call(
        functools.partial(place_body, nh), 1, ins, [smem()] + [whole(a) for a in pieces],
        outs, [whole(outs[0])], name="place",
    )
    shared_grad = table.reshape(layers, depth, both)
    dt_grad = step_sums[:, :heads_here].transpose(0, 2, 1)
    back = lambda parts: jnp.concatenate(parts, axis=0).transpose(1, 0, 2)
    return (
        back(x_res),
        back(grad_res),
        gain_grad,
        jnp.stack([e[1] for e in early_grads]).astype(F32),
        jnp.stack(late_grads).astype(F32),
        shared_grad,
        dt_grad,
        conv_total[:, :taps],
        conv_total[:, taps],
        conv_shared[:, :taps],
        conv_shared[:, taps],
        head_total[:, 0, :heads_here],
        head_total[:, 1, :heads_here],
        jnp.sum(chan_total[:, 1].reshape(layers, heads_here, size), axis=-1),
        chan_total[:, 0],
        jnp.stack([e[0] for e in early_grads]).astype(F32),
    )


def solution(mesh):
    rows = P(("seq", "heads"), None, None)
    placed = (
        rows, rows, P(), P(None, "seq"), P(None, "seq", "heads"), P(None, "seq", "heads"),
        P(None, "seq", None), P(None, "seq", "heads"), P(None, None, "heads"), P(None, "heads"), P(), P(),
        P(None, "heads"), P(None, "heads"), P(None, "heads"), P(None, "heads"), P(None, "heads", "seq"),
    )
    made = (
        rows, rows, P(None, "seq"), P(None, "seq", "heads"), P(None, "seq", "heads"),
        P(None, "seq", None), P(None, "seq", "heads"), P(None, None, "heads"), P(None, "heads"), P(), P(),
        P(None, "heads"), P(None, "heads"), P(None, "heads"), P(None, "heads"), P(None, "heads", "seq"),
    )
    return jax.shard_map(shards, mesh=mesh, in_specs=placed, out_specs=made, check_vma=False)
```
